512 devices in a mesh: pair: 32 (over z, core), aux: 16 (over x, y).
Axes of the slice: x: 4, y: 4, z: 16, core: 2. Of those that a mesh axis runs over, the one named last changes fastest.
Arguments:
- tiles: bfloat16 [5632, 64, 3328], P(('pair', 'aux')), may hold values from -6 to 6
- coeff: bfloat16 [4096, 256], P('pair'), may hold values from -0.375 to 0.375
- support: int32 [64, 48], P('pair'), may hold values from 0 to 255, all different within a row
- row_block: int32 [5632], P(('pair', 'aux')), may hold values from 0 to 1
- col_block: int32 [5632], P(('pair', 'aux')), may hold values from 0 to 63
- owner: int32 [5632, 1], P(('pair', 'aux')), may hold values from 0 to 15; in each aligned block of 11 rows (0 to 10, 11 to 21, ...) at most 2 rows name the same one
- local_block: int32 [5632], P(('pair', 'aux')), may hold values from 0 to 31
- metric: bfloat16 [512, 52, 52], P('aux'), may hold values from -0.015625 to 0.015625
Outputs:
- exchange: float32 [64, 64, 64], P('pair', 'aux')
The draws below stay inside these ranges and needn't reach their ends.
Inputs may be any that keep to these rules, and one draw needn't show every extreme that they name: Within the 11 tiles of one device no owner appears more than 2 times; some device names one owner exactly 2 times. `support`: the 48 orbitals of one row are distinct; every orbital appears in some row.
All inputs are finite; a program needn't handle non-finite values.
Results may differ from the reference program's by a relative error of at most 0.0038.
Values may be sent and summed in bfloat16 or wider, within the bound.
No kernel may reach another device: no remote copies, remote signals or barrier semaphores. Data moves between devices by JAX's collectives and lax.ppermute only.
A program may use at most 64 MiB of HBM per device.

```python
import math
import jax
import jax.numpy as jnp
import numpy as np
from jax import lax

W = 64
AW = 52
NOCC = 256
NSUP = 48
KI = 11
BLKS = 2
QDEV = 32
CAP = 2
NBLK = 64
NB = 4096
NQ = 512
ITEMS = 5632
N_AUX = 16


def plant(drawn, rng, smallest, high):
    place = [jax.random.randint(jax.random.fold_in(rng, axis), (), 0, length) for axis, length in enumerate(drawn.shape)]
    main_axis = drawn.shape.index(max(drawn.shape))
    beside = place[:main_axis] + [(place[main_axis] + 1) % drawn.shape[main_axis]] + place[main_axis + 1:]
    return drawn.at[tuple(place)].set(smallest).at[tuple(beside)].set(high)


def levels(stream_key, extent, cuts, low, high):
    gain = 1.0
    for position, parts in cuts:
        draws = jax.random.uniform(jax.random.fold_in(jax.random.fold_in(stream_key, 6), position), (parts,), jnp.float32, low / len(cuts), high / len(cuts))
        gain = gain * jnp.repeat(jnp.exp(draws), extent[position] // parts).reshape((-1,) + (1,) * (len(extent) - 1 - position))
    return gain


def choose_distinct(key, rows, count, top, lift):
    ranking = jax.random.permutation(jax.random.fold_in(key, 1), count)
    favour = ranking
    for power in range(3):
        favour = favour * favour // count
    favour = favour * lift // count
    chance = jax.random.randint(jax.random.fold_in(key, 2), (rows, count), 0, 4096) + favour
    holders = jax.random.permutation(jax.random.fold_in(key, 3), rows)[jnp.arange(count) % rows]
    chance = jnp.where(jnp.arange(rows)[:, None] == holders[None, :], 1 << 14, chance)
    merit = chance * count + jnp.arange(count)
    return lax.top_k(merit.astype(jnp.int32), top)[1].astype(jnp.int32)


def assign_block(rng, own, number, rows, count, top, limit, lean):
    sequence = jax.random.permutation(rng, count)
    packed, common = shares(count, rows * top, limit, lean, True), shares(count, rows * top, limit, lean, False)
    places = jnp.arange(count)

    def named(lengths, turn):
        used = int((lengths > 0).sum())
        fixed = max(1, used // 4)
        shifted = fixed + (places - fixed + turn * (used - fixed)) % max(1, count - fixed)
        return jnp.zeros((count,), jnp.int32).at[sequence[jnp.where(places < fixed, places, shifted)]].set(jnp.asarray(lengths, jnp.int32))

    lengths = jnp.where(number % 4 == 0, named(packed, number // 4), named(common, number - number // 4 - 1))
    mixed = jax.random.permutation(jax.random.fold_in(own, 3), count)
    donor, taker = mixed[0:count // 2 * 2:2], mixed[1:count // 2 * 2:2]
    margin = jnp.minimum(lengths[donor] - 1, limit - lengths[taker]) // 2
    margin = jnp.where((donor == sequence[0]) | (taker == sequence[0]) | (lengths[taker] == 0), 0, jnp.maximum(margin, 0))
    shifted = jax.random.randint(jax.random.fold_in(own, 4), (count // 2,), 0, 1 << 20) % (margin + 1)
    lengths = lengths.at[donor].add(-shifted).at[taker].add(shifted)
    items = jnp.searchsorted(jnp.cumsum(lengths), jnp.arange(rows * top), side="right").astype(jnp.int32)
    grid = items.reshape(top, rows).T
    grid = grid[jax.random.permutation(jax.random.fold_in(own, 1), rows)]
    turn = jax.random.randint(jax.random.fold_in(own, 2), (rows, 1), 0, top)
    return jnp.take_along_axis(grid, (jnp.arange(top)[None, :] + turn) % top, axis=1)


def shares(amount, total, reach, lean, full):
    loads = [(1 << 20) // math.isqrt(grade ** lean) + 1 for grade in range(1, amount + 1)]
    largest = reach if full else min(reach, max(-(-total // amount), total * loads[0] // sum(loads)))
    least = 1 if total - largest >= amount - 1 else 0
    given, surplus = [largest] + [least] * (amount - 1), total - largest - least * (amount - 1)
    while surplus > 0:
        movable = [i for i in range(1, amount) if given[i] < largest] or [i for i in range(1, amount) if given[i] < reach]
        mass, budget = sum([loads[i] for i in movable]), surplus
        for i in movable:
            more = min(reach - given[i], max(1, budget * loads[i] // mass), surplus)
            given[i] = given[i] + more
            surplus = surplus - more
    return np.array(given)


def noise(stream_key, shape, scale, most, shards=(), kind=jnp.bfloat16):
    array = jax.random.normal(stream_key, shape, jnp.float32) * scale
    if len(shards) > 0:
        array = levels(stream_key, shape, shards, -0.22, 0.18) * array
    return jnp.clip(array, min=-most, max=most).astype(kind)


def setup_inputs(seed: int = 0) -> dict:
    arg_keys = jax.random.split(jax.random.key(seed), 9)
    tiles = noise(arg_keys[0], (ITEMS, W, W * AW), 1.0, 6.0, ((0, 512),))
    coeff = noise(arg_keys[1], (NB, NOCC), (4 * W) ** -0.5, 0.375, ((0, 32),))
    support = choose_distinct(arg_keys[2], NBLK, NOCC, NSUP, 0)
    row_block = plant(jax.random.randint(arg_keys[3], (ITEMS,), 0, BLKS), jax.random.fold_in(arg_keys[3], 1), 0, BLKS - 1).astype(jnp.int32)
    col_block = plant(jax.random.randint(arg_keys[4], (ITEMS,), 0, NBLK), jax.random.fold_in(arg_keys[4], 1), 0, NBLK - 1).astype(jnp.int32)
    owner_keys = jax.random.split(jax.random.fold_in(arg_keys[5], 1), ITEMS // KI)
    owner_turns = jax.random.permutation(jax.random.fold_in(arg_keys[5], 3), ITEMS // KI)
    owner = jax.vmap(lambda own, number: assign_block(jax.random.fold_in(arg_keys[5], 2), own, number, KI, N_AUX, 1, CAP, 2))(owner_keys, owner_turns).reshape((ITEMS, 1))
    local_block = plant(jax.random.randint(arg_keys[6], (ITEMS,), 0, QDEV), jax.random.fold_in(arg_keys[6], 1), 0, QDEV - 1).astype(jnp.int32)
    metric = noise(arg_keys[7], (NQ, AW, AW), (64 * NSUP * AW) ** -0.5, 0.015625, ((0, 16),))
    return dict(tiles=tiles, coeff=coeff, support=support, row_block=row_block, col_block=col_block, owner=owner, local_block=local_block, metric=metric)


def reference(tiles, coeff, support, row_block, col_block, owner, local_block, metric):
    block_total = coeff.shape[0] // W
    coeff_blocks = coeff.reshape(block_total, W, NOCC)
    device_total = tiles.shape[0] // KI

    def step(carry, device):
        start = device * KI
        part_tiles = lax.dynamic_slice_in_dim(tiles, start, KI, 0)
        part_rows = lax.dynamic_slice_in_dim(row_block, start, KI, 0)
        part_cols = lax.dynamic_slice_in_dim(col_block, start, KI, 0)
        part_owner = lax.dynamic_slice_in_dim(owner, start, KI, 0)
        part_local = lax.dynamic_slice_in_dim(local_block, start, KI, 0)
        mu_block = ((device // N_AUX) * BLKS + part_rows).astype(jnp.int32)
        coeff_rows = coeff_blocks[mu_block]
        picked = support[mu_block]
        coeffs = jnp.take_along_axis(coeff_rows, picked[:, None, :], axis=2)
        halves = jnp.einsum("kms,kmx->ksx", coeffs.astype(jnp.float32), part_tiles.astype(jnp.float32)).astype(jnp.bfloat16)
        aux_block = (part_owner[:, 0] * QDEV + part_local).astype(jnp.int32)
        metric_tiles = metric[aux_block]
        shaped = halves.reshape(KI, NSUP, W, AW)
        fitted = jnp.einsum("ksnp,kpq->ksnq", shaped.astype(jnp.float32), metric_tiles.astype(jnp.float32)).astype(jnp.bfloat16)
        block_sums = jnp.einsum("ksnp,ksmp->knm", shaped.astype(jnp.float32), fitted.astype(jnp.float32)).reshape(KI, W * W)
        onehot = (part_cols[:, None] == jnp.arange(block_total, dtype=jnp.int32)[None, :]).astype(jnp.float32)
        added = jnp.einsum("kb,kx->bx", onehot, block_sums, precision=lax.Precision.HIGHEST)
        return carry - added, None

    init = jnp.zeros((block_total, W * W), jnp.float32)
    summed, _ = lax.scan(step, init, jnp.arange(device_total, dtype=jnp.int32))
    return summed.reshape(block_total, W, W)
```

```python
import functools
import jax
import jax.numpy as jnp
from jax import lax
from jax.experimental import pallas as pl
from jax.experimental.pallas import tpu as pltpu
from jax.sharding import PartitionSpec as P

LANES = 128
HALF = 64
SLOTS = 8


def request_kernel(owner_ref, local_ref, col_ref, out_ref):
    aux_count = out_ref.shape[0]
    shape = (aux_count, owner_ref.shape[1])
    position = lax.broadcasted_iota(jnp.int32, shape, 1)
    match = owner_ref[...] == lax.broadcasted_iota(jnp.int32, shape, 0)
    local = jnp.broadcast_to(local_ref[...], shape)
    first = jnp.min(jnp.where(match, position, LANES), axis=1, keepdims=True)
    last = jnp.max(jnp.where(match, position, -1), axis=1, keepdims=True)
    out_ref[...] = jnp.zeros_like(out_ref)
    out_ref[:, 0:1] = jnp.sum(jnp.where(position == first, local, 0), axis=1, keepdims=True)
    out_ref[:, 1:2] = jnp.sum(jnp.where(position == last, local, 0), axis=1, keepdims=True)
    out_ref[:, 32 : 32 + shape[1]] = jnp.broadcast_to(col_ref[...], shape)


def half_kernel(row_ref, tile_ref, coeff_ref, support_ref, out_ref, picked, half, slabs):
    width = tile_ref.shape[1]
    orbitals = support_ref.shape[1]
    groups = orbitals // 2
    aux_width = tile_ref.shape[2] // width

    @pl.when(pl.program_id(0) == 0)
    def _():
        for block in range(support_ref.shape[0]):
            shape = (coeff_ref.shape[1], orbitals)
            onehot = support_ref[block : block + 1, :] == lax.broadcasted_iota(jnp.int32, shape, 0)
            chosen = jnp.dot(
                coeff_ref[block * width : (block + 1) * width, :],
                onehot.astype(jnp.float32).astype(jnp.bfloat16),
                preferred_element_type=jnp.float32,
            )
            picked[block] = chosen.T.astype(jnp.bfloat16)

    half[...] = jnp.dot(
        picked[row_ref[pl.program_id(0)]], tile_ref[0], preferred_element_type=jnp.float32
    )
    lane = lax.broadcasted_iota(jnp.int32, (orbitals, LANES), 1)
    low = lane[:groups] < HALF
    for nu in range(width):
        start = nu * aux_width
        base, shift = start // LANES * LANES, start % LANES
        window = half[:, base : base + LANES]
        if shift + aux_width > LANES:
            window = jnp.where(lane >= shift, window, half[:, base + LANES : base + 2 * LANES])
        first, second = window[:groups], window[groups:]
        if shift:
            first = pltpu.roll(first, LANES - shift, 1)
        if shift != HALF:
            second = pltpu.roll(second, (LANES + HALF - shift) % LANES, 1)
        slabs[nu * groups : (nu + 1) * groups, :] = jnp.where(low, first, second)
    for g in range(groups):
        out_ref[0, g * width : (g + 1) * width, :] = slabs[
            pl.ds(g, width, stride=groups), :
        ].astype(jnp.bfloat16)


def serve_kernel(asked_ref, metric_ref, out_ref):
    lane = lax.broadcasted_iota(jnp.int32, out_ref.shape[1:], 1)
    for peer in range(out_ref.shape[0]):
        out_ref[peer] = jnp.where(
            lane < HALF, metric_ref[asked_ref[peer, 0]], metric_ref[asked_ref[peer, 1]]
        )


def term_kernel(owner_ref, first_ref, second_ref, metric_ref, out_ref, total):
    pair = pl.program_id(0)
    item_count = owner_ref.shape[0]
    width = metric_ref.shape[1]
    groups = first_ref.shape[1] // width
    lane = lax.broadcasted_iota(jnp.int32, (width, LANES), 1)

    def placed(item):
        mine = owner_ref[item]
        slot = jnp.int32(0)
        for other in range(item_count):
            slot = slot | jnp.where((owner_ref[other] == mine) & (other < item), 1, 0)
        block = metric_ref[mine].astype(jnp.float32)
        turned = pltpu.roll(block, HALF, 1)
        low = jnp.where(slot == 0, block, turned)
        high = jnp.where(slot == 0, turned, block)
        stacked = [jnp.where(lane < HALF, low, 0.0), jnp.where(lane < HALF, 0.0, high)]
        return jnp.concatenate(stacked, axis=0).astype(jnp.bfloat16)

    @pl.when(pair == 0)
    def _():
        total[...] = jnp.zeros_like(total)

    gap = item_count - pl.num_programs(0)
    metric_a, metric_b = placed(pair), placed(pair + gap)
    zero = jnp.zeros_like(metric_a)
    metrics = jnp.concatenate(
        [jnp.concatenate([metric_a, zero], axis=1), jnp.concatenate([zero, metric_b], axis=1)],
        axis=0,
    )
    halves = jnp.concatenate([first_ref[0], second_ref[0]], axis=1)
    fitted = jnp.dot(halves, metrics, preferred_element_type=jnp.float32).astype(jnp.bfloat16)

    def spread(array):
        rows = [
            jnp.concatenate(
                [
                    array[g * width : (g + 1) * width, side * LANES : (side + 1) * LANES]
                    for g in range(groups)
                ],
                axis=1,
            )
            for side in range(2)
        ]
        return jnp.concatenate(rows, axis=0)

    product = lax.dot_general(
        spread(halves),
        spread(fitted),
        (((1,), (1,)), ((), ())),
        preferred_element_type=jnp.float32,
    )
    total[pl.ds(pair, width, stride=SLOTS), :] = jnp.where(
        lane < HALF, product[:width], product[width:]
    )

    @pl.when(pair == pl.num_programs(0) - 1)
    def _():
        out_ref[...] = total[...].astype(jnp.bfloat16)


def combine_kernel(parts_ref, pick_ref, out_ref):
    sources = parts_ref.shape[0]
    rows = parts_ref.shape[1] // SLOTS
    pairs = pick_ref.shape[0] // 8
    low = lax.broadcasted_iota(jnp.int32, (pairs, LANES), 1) < HALF
    for step in range(rows // 2):
        block = parts_ref[:, step * 2 * SLOTS : (step + 1) * 2 * SLOTS, :]
        summed = jnp.dot(
            pick_ref[...],
            block.reshape(sources * 2 * SLOTS, LANES),
            preferred_element_type=jnp.float32,
        )
        for parity in range(2):
            at = parity * 4 * pairs
            even = summed[at : at + pairs] + pltpu.roll(summed[at + pairs : at + 2 * pairs], HALF, 1)
            odd = summed[at + 3 * pairs : at + 4 * pairs] + pltpu.roll(
                summed[at + 2 * pairs : at + 3 * pairs], HALF, 1
            )
            out_ref[pl.ds(step * 2 + parity, pairs, stride=rows), :] = jnp.where(low, even, odd)


def final_kernel(parts_ref, out_ref):
    rows = out_ref.shape[1]
    summed = jnp.sum(parts_ref[...], axis=0)
    for side in range(out_ref.shape[0]):
        out_ref[side] = summed[:, side * HALF : (side + 1) * HALF]


def shards(tiles, coeff, support, row_block, col_block, owner, local_block, metric):
    item_count, width, columns = tiles.shape
    aux_width = metric.shape[1]
    orbitals = support.shape[1]
    aux_count = lax.axis_size("aux")
    pair_count = lax.axis_size("pair")
    groups = orbitals // 2
    pair_steps = (item_count + 1) // 2
    gap = item_count - pair_steps
    vmem = pl.BlockSpec(memory_space=pltpu.VMEM)
    smem = pl.BlockSpec(memory_space=pltpu.SMEM)
    row = lambda array: array.reshape(1, item_count)

    request = pl.pallas_call(
        request_kernel,
        out_shape=jax.ShapeDtypeStruct((aux_count, LANES), jnp.int32),
        in_specs=[vmem] * 3,
        out_specs=vmem,
        name="request",
    )(row(owner), row(local_block), row(col_block))
    asked = lax.all_to_all(
        request.reshape(aux_count, 1, LANES), "aux", split_axis=0, concat_axis=0, tiled=True
    ).reshape(aux_count, LANES)

    halves = pl.pallas_call(
        half_kernel,
        grid_spec=pltpu.PrefetchScalarGridSpec(
            num_scalar_prefetch=1,
            grid=(item_count,),
            in_specs=[
                pl.BlockSpec((1, width, columns), lambda k, rows: (k, 0, 0)),
                pl.BlockSpec(coeff.shape, lambda k, rows: (0, 0)),
                pl.BlockSpec(support.shape, lambda k, rows: (0, 0)),
            ],
            out_specs=pl.BlockSpec((1, groups * width, LANES), lambda k, rows: (k, 0, 0)),
            scratch_shapes=[
                pltpu.VMEM((support.shape[0], orbitals, width), jnp.bfloat16),
                pltpu.VMEM((orbitals, columns), jnp.float32),
                pltpu.VMEM((groups * width, LANES), jnp.float32),
            ],
        ),
        out_shape=jax.ShapeDtypeStruct((item_count, groups * width, LANES), jnp.bfloat16),
        cost_estimate=pl.CostEstimate(
            flops=2 * item_count * orbitals * width * columns,
            bytes_accessed=2 * item_count * (width * columns + groups * width * LANES),
            transcendentals=0,
        ),
        name="half",
    )(row_block, tiles, coeff, support)

    side = jnp.pad(metric, ((0, 0), (0, width - aux_width), (0, HALF - aux_width)))
    padded = jnp.concatenate([side, side], axis=2)
    served = pl.pallas_call(
        serve_kernel,
        out_shape=jax.ShapeDtypeStruct((aux_count, width, LANES), jnp.bfloat16),
        in_specs=[smem, vmem],
        out_specs=vmem,
        name="serve",
    )(asked, padded)
    metric_tiles = lax.all_to_all(served, "aux", split_axis=0, concat_axis=0, tiled=True)

    cols = asked[:, 32 : 32 + item_count]
    fill = ((0, 0), (0, SLOTS - pair_steps))
    cols_a = jnp.pad(cols[:, :pair_steps], fill, constant_values=-1)
    cols_b = jnp.pad(cols[:, gap:], fill, constant_values=-1)
    cols_b = jnp.where(jnp.arange(SLOTS)[None, :] < pair_steps - gap, -1, cols_b)
    spread = lambda array: jnp.broadcast_to(array[:, None, :], (aux_count, 2, SLOTS)).reshape(1, -1)
    place = jnp.arange(8 * pair_count, dtype=jnp.int32)[:, None]
    block = 2 * (place % pair_count) + place // (2 * pair_count) % 2
    side_b = place // pair_count % 2 == 1
    parity = jnp.arange(aux_count * 2 * SLOTS, dtype=jnp.int32)[None, :] // SLOTS % 2
    hit = jnp.where(side_b, spread(cols_b) == block, spread(cols_a) == block)
    pick = jnp.where(hit & (parity == place // (4 * pair_count)), -1.0, 0.0).astype(jnp.bfloat16)

    blocks = pl.pallas_call(
        term_kernel,
        grid_spec=pltpu.PrefetchScalarGridSpec(
            num_scalar_prefetch=1,
            grid=(pair_steps,),
            in_specs=[
                pl.BlockSpec((1, groups * width, LANES), lambda t, own: (t, 0, 0)),
                pl.BlockSpec((1, groups * width, LANES), lambda t, own: (t + gap, 0, 0)),
                pl.BlockSpec((aux_count, width, LANES), lambda t, own: (0, 0, 0)),
            ],
            out_specs=pl.BlockSpec((width * SLOTS, LANES), lambda t, own: (0, 0)),
            scratch_shapes=[pltpu.VMEM((width * SLOTS, LANES), jnp.float32)],
        ),
        out_shape=jax.ShapeDtypeStruct((width * SLOTS, LANES), jnp.bfloat16),
        compiler_params=pltpu.CompilerParams(vmem_limit_bytes=32 * 1024 * 1024),
        name="term",
    )(owner.reshape(item_count), halves, halves, metric_tiles)
    rows = width // aux_count
    parts = lax.all_to_all(
        blocks.reshape(aux_count, rows * SLOTS, LANES), "aux", split_axis=0, concat_axis=0, tiled=True
    )

    sums = pl.pallas_call(
        combine_kernel,
        out_shape=jax.ShapeDtypeStruct((pair_count * rows, LANES), jnp.float32),
        in_specs=[vmem] * 2,
        out_specs=vmem,
        name="combine",
    )(parts, pick)
    arrived = lax.all_to_all(
        sums.reshape(pair_count, rows, LANES), "pair", split_axis=0, concat_axis=0, tiled=True
    )
    return pl.pallas_call(
        final_kernel,
        out_shape=jax.ShapeDtypeStruct((2, rows, width), jnp.float32),
        in_specs=[vmem],
        out_specs=vmem,
        name="final",
    )(arrived)


def solution(mesh):
    return jax.shard_map(
        shards,
        mesh=mesh,
        in_specs=(
            P(("pair", "aux"), None, None),
            P("pair", None),
            P("pair", None),
            P(("pair", "aux")),
            P(("pair", "aux")),
            P(("pair", "aux"), None),
            P(("pair", "aux")),
            P("aux", None, None),
        ),
        out_specs=P("pair", "aux", None),
        check_vma=False,
    )
```

```python
import jax
import jax.numpy as jnp
from jax import lax
from jax.experimental import pallas as pl
from jax.experimental.pallas import tpu as pltpu
from jax.sharding import PartitionSpec as P

LANES = 128
HALF = 64
MIB = 1 << 20
EARLY_LIMIT = 61_000_000
SERVE_LIMIT = 55_700_000
LATE_LIMIT = 51_000_000
TERM_LIMIT = 51_000_000
SLOTS = 8


def request_kernel(owner_ref, local_ref, col_ref, out_ref):
    aux_count = out_ref.shape[0]
    shape = (aux_count, owner_ref.shape[1])
    position = lax.broadcasted_iota(jnp.int32, shape, 1)
    match = owner_ref[...] == lax.broadcasted_iota(jnp.int32, shape, 0)
    local = jnp.broadcast_to(local_ref[...], shape)
    first = jnp.min(jnp.where(match, position, LANES), axis=1, keepdims=True)
    last = jnp.max(jnp.where(match, position, -1), axis=1, keepdims=True)
    out_ref[...] = jnp.zeros_like(out_ref)
    out_ref[:, 0:1] = jnp.sum(jnp.where(position == first, local, 0), axis=1, keepdims=True)
    out_ref[:, 1:2] = jnp.sum(jnp.where(position == last, local, 0), axis=1, keepdims=True)
    out_ref[:, 32 : 32 + shape[1]] = jnp.broadcast_to(col_ref[...], shape)


def place(metric_ref, coeff_ref, support_ref, padded_ref, picked_ref, rows_ref):
    aux_width, blocks, _ = metric_ref.shape
    width = coeff_ref.shape[0] // support_ref.shape[0]
    shape = (coeff_ref.shape[1], support_ref.shape[1])
    for block in range(support_ref.shape[0]):
        onehot = support_ref[block : block + 1, :] == lax.broadcasted_iota(jnp.int32, shape, 0)
        chosen = jnp.dot(
            coeff_ref[block * width : (block + 1) * width, :],
            onehot.astype(jnp.float32).astype(jnp.bfloat16),
            preferred_element_type=jnp.float32,
        )
        picked_ref[block] = chosen.T.astype(jnp.bfloat16)
    rows_ref[...] = jnp.zeros_like(rows_ref)
    for p in range(aux_width):
        rows_ref[p * blocks : (p + 1) * blocks, :aux_width] = metric_ref[p].astype(jnp.float32)
    padded_ref[...] = jnp.zeros_like(padded_ref)
    for block in range(blocks):
        entry = rows_ref[pl.ds(block, aux_width, stride=blocks), :]
        padded_ref[block, :aux_width, :] = (entry + pltpu.roll(entry, HALF, 1)).astype(jnp.bfloat16)


def fetch(tile_ref, first, buffer_ref, sems):
    copies = [
        pltpu.make_async_copy(tile_ref.at[first + item], buffer_ref.at[item], sems.at[item])
        for item in range(buffer_ref.shape[0])
    ]
    for copy in copies:
        copy.start()
    return copies


def half_tiles(row_ref, first, picked_ref, copies, buffer_ref, half_ref, slab_ref, put):
    item_count, width, columns = buffer_ref.shape
    orbitals = picked_ref.shape[1]
    groups = orbitals // 2
    aux_width = columns // width
    lane = lax.broadcasted_iota(jnp.int32, (orbitals, LANES), 1)
    low = lane[:groups] < HALF

    def multiply(item):
        copies[item].wait()
        half_ref[item % 2] = jnp.dot(
            picked_ref[row_ref[first + item]], buffer_ref[item], preferred_element_type=jnp.float32
        )

    multiply(0)
    for item in range(item_count):
        if item + 1 < item_count:
            multiply(item + 1)
        half, slabs = half_ref.at[item % 2], slab_ref.at[item % 2]
        for nu in range(width):
            start = nu * aux_width
            base, shift = start // LANES * LANES, start % LANES
            window = half[:, base : base + LANES]
            if shift + aux_width > LANES:
                window = jnp.where(lane >= shift, window, half[:, base + LANES : base + 2 * LANES])
            front, back = window[:groups], window[groups:]
            if shift:
                front = pltpu.roll(front, LANES - shift, 1)
            if shift != HALF:
                back = pltpu.roll(back, (LANES + HALF - shift) % LANES, 1)
            slabs[nu * groups : (nu + 1) * groups, :] = jnp.where(low, front, back)
        for g in range(groups):
            put(item, g * width, slabs[pl.ds(g, width, stride=groups), :].astype(jnp.bfloat16))


def early_kernel(row_ref, tile_ref, metric_ref, coeff_ref, support_ref, *refs):
    out_ref, padded_ref, picked_ref, rows_ref, made_ref, buffer_ref, half_ref, slab_ref, sems = refs
    count = buffer_ref.shape[0]
    first = tile_ref.shape[0] - count
    copies = fetch(tile_ref, first, buffer_ref, sems)
    place(metric_ref, coeff_ref, support_ref, padded_ref, picked_ref, rows_ref)
    sends = [
        pltpu.make_async_copy(made_ref.at[item], out_ref.at[item], sems.at[count + item])
        for item in range(count)
    ]

    def put(item, at, rows):
        made_ref[item, at : at + rows.shape[0], :] = rows
        if at + rows.shape[0] == made_ref.shape[1]:
            sends[item].start()

    half_tiles(row_ref, first, picked_ref, copies, buffer_ref, half_ref, slab_ref, put)
    for send in sends:
        send.wait()


def late_kernel(row_ref, tile_ref, picked_ref, out_ref, buffer_ref, half_ref, slab_ref, sems):
    copies = fetch(tile_ref, 0, buffer_ref, sems)

    def put(item, at, rows):
        out_ref[item, at : at + rows.shape[0], :] = rows

    half_tiles(row_ref, 0, picked_ref, copies, buffer_ref, half_ref, slab_ref, put)


def serve_kernel(asked_ref, metric_ref, out_ref):
    lane = lax.broadcasted_iota(jnp.int32, out_ref.shape[1:], 1)
    for peer in range(out_ref.shape[0]):
        out_ref[peer] = jnp.where(
            lane < HALF, metric_ref[asked_ref[peer, 0]], metric_ref[asked_ref[peer, 1]]
        )


def term_kernel(owner_ref, late_ref, early_ref, metric_ref, out_ref, total):
    late_count, rows, _ = late_ref.shape
    item_count = late_count + early_ref.shape[0]
    width = out_ref.shape[0] // SLOTS
    depth = metric_ref.shape[1]
    steps = (item_count + 1) // 2
    gap = item_count - steps
    groups = rows // width
    lane = lax.broadcasted_iota(jnp.int32, (depth, LANES), 1)
    rest = jnp.zeros((HALF - depth, LANES), jnp.float32)

    def placed(item):
        mine = owner_ref[item]
        slot = jnp.int32(0)
        for other in range(item):
            slot = slot | jnp.where(owner_ref[other] == mine, 1, 0)
        block = metric_ref[mine].astype(jnp.float32)
        turned = pltpu.roll(block, HALF, 1)
        low = jnp.where(slot == 0, block, turned)
        high = jnp.where(slot == 0, turned, block)
        stacked = [jnp.where(lane < HALF, low, 0.0), rest, jnp.where(lane < HALF, 0.0, high), rest]
        return jnp.concatenate(stacked, axis=0).astype(jnp.bfloat16)

    def spread(array):
        return jnp.concatenate(
            [array[g * width : (g + 1) * width, :] for g in range(groups)], axis=1
        )

    def term(item):
        halves = late_ref[item] if item < late_count else early_ref[item - late_count]
        fitted = jnp.dot(halves, placed(item), preferred_element_type=jnp.float32)
        return lax.dot_general(
            spread(halves),
            spread(fitted.astype(jnp.bfloat16)),
            (((1,), (1,)), ((), ())),
            preferred_element_type=jnp.float32,
        )

    total[...] = jnp.zeros_like(total)
    terms = []
    for item in range(item_count):
        terms.append(term(item))
        if item >= gap and item - gap < steps:
            at = item - gap
            total[pl.ds(at, width, stride=SLOTS), :] = jnp.concatenate(
                [terms[at], terms[item]], axis=1
            )
    out_ref[...] = total[...].astype(jnp.bfloat16)


def combine_kernel(parts_ref, pick_ref, out_ref):
    sources = parts_ref.shape[0]
    rows = parts_ref.shape[1] // SLOTS
    pairs = pick_ref.shape[0] // 8
    low = lax.broadcasted_iota(jnp.int32, (pairs, LANES), 1) < HALF
    for step in range(rows // 2):
        block = parts_ref[:, step * 2 * SLOTS : (step + 1) * 2 * SLOTS, :]
        summed = jnp.dot(
            pick_ref[...],
            block.reshape(sources * 2 * SLOTS, LANES),
            preferred_element_type=jnp.float32,
        )
        for parity in range(2):
            at = parity * 4 * pairs
            even = summed[at : at + pairs] + pltpu.roll(summed[at + pairs : at + 2 * pairs], HALF, 1)
            odd = summed[at + 3 * pairs : at + 4 * pairs] + pltpu.roll(
                summed[at + 2 * pairs : at + 3 * pairs], HALF, 1
            )
            out_ref[pl.ds(step * 2 + parity, pairs, stride=rows), :] = jnp.where(low, even, odd)


def final_kernel(parts_ref, out_ref):
    rows = out_ref.shape[1]
    summed = jnp.sum(parts_ref[...], axis=0)
    for side in range(out_ref.shape[0]):
        out_ref[side] = summed[:, side * HALF : (side + 1) * HALF]


def shards(tiles, coeff, support, row_block, col_block, owner, local_block, metric):
    item_count, width, columns = tiles.shape
    aux_width = metric.shape[1]
    orbitals = support.shape[1]
    aux_count = lax.axis_size("aux")
    pair_count = lax.axis_size("pair")
    groups = orbitals // 2
    pair_steps = (item_count + 1) // 2
    gap = item_count - pair_steps
    vmem = pl.BlockSpec(memory_space=pltpu.VMEM)
    smem = pl.BlockSpec(memory_space=pltpu.SMEM)
    anywhere = pl.BlockSpec(memory_space=pl.ANY)
    small = pltpu.CompilerParams(vmem_limit_bytes=8 * MIB)
    row = lambda array: array.reshape(1, item_count)

    request = pl.pallas_call(
        request_kernel,
        out_shape=jax.ShapeDtypeStruct((aux_count, LANES), jnp.int32),
        in_specs=[vmem] * 3,
        out_specs=vmem,
        name="request",
    )(row(owner), row(local_block), row(col_block))
    asked = lax.all_to_all(
        request.reshape(aux_count, 1, LANES), "aux", split_axis=0, concat_axis=0, tiled=True
    ).reshape(aux_count, LANES)

    late_rows = groups * width
    by_aux = metric.transpose(1, 0, 2)
    depth = -(-aux_width // 8) * 8
    early_count = item_count * 4 // 11
    late_count = item_count - early_count

    def half_scratch(count):
        return [
            pltpu.VMEM((count, width, columns), jnp.bfloat16),
            pltpu.VMEM((2, orbitals, columns), jnp.float32),
            pltpu.VMEM((2, late_rows, LANES), jnp.float32),
            pltpu.SemaphoreType.DMA((2 * count,)),
        ]

    def cost(count):
        return pl.CostEstimate(
            flops=2 * count * orbitals * width * columns,
            bytes_accessed=2 * count * (width * columns + late_rows * LANES),
            transcendentals=0,
        )

    early, padded, picked = pl.pallas_call(
        early_kernel,
        out_shape=[
            jax.ShapeDtypeStruct((early_count, late_rows, LANES), jnp.bfloat16),
            jax.ShapeDtypeStruct((metric.shape[0], depth, LANES), jnp.bfloat16),
            jax.ShapeDtypeStruct((support.shape[0], orbitals, width), jnp.bfloat16),
        ],
        in_specs=[smem, anywhere, vmem, vmem, vmem],
        out_specs=[anywhere, vmem, vmem],
        scratch_shapes=[
            pltpu.VMEM((aux_width * metric.shape[0], LANES), jnp.float32),
            pltpu.VMEM((early_count, late_rows, LANES), jnp.bfloat16),
        ]
        + half_scratch(early_count),
        compiler_params=pltpu.CompilerParams(vmem_limit_bytes=EARLY_LIMIT),
        cost_estimate=cost(early_count),
        name="early",
    )(row_block, tiles, by_aux, coeff, support)

    served = pl.pallas_call(
        serve_kernel,
        out_shape=jax.ShapeDtypeStruct((aux_count, depth, LANES), jnp.bfloat16),
        in_specs=[smem, vmem],
        out_specs=vmem,
        compiler_params=pltpu.CompilerParams(vmem_limit_bytes=SERVE_LIMIT),
        name="serve",
    )(asked, padded)
    metric_tiles = lax.all_to_all(served, "aux", split_axis=0, concat_axis=0, tiled=True)

    picked, _ = lax.optimization_barrier((picked, served))
    late = pl.pallas_call(
        late_kernel,
        out_shape=jax.ShapeDtypeStruct((late_count, late_rows, LANES), jnp.bfloat16),
        in_specs=[smem, anywhere, vmem],
        out_specs=vmem,
        scratch_shapes=half_scratch(late_count),
        compiler_params=pltpu.CompilerParams(vmem_limit_bytes=LATE_LIMIT),
        cost_estimate=cost(late_count),
        name="late",
    )(row_block, tiles, picked)

    cols = asked[:, 32 : 32 + item_count]
    fill = ((0, 0), (0, SLOTS - pair_steps))
    cols_a = jnp.pad(cols[:, :pair_steps], fill, constant_values=-1)
    cols_b = jnp.pad(cols[:, gap:], fill, constant_values=-1)
    cols_b = jnp.where(jnp.arange(SLOTS)[None, :] < pair_steps - gap, -1, cols_b)
    spread = lambda array: jnp.broadcast_to(array[:, None, :], (aux_count, 2, SLOTS)).reshape(1, -1)
    place = jnp.arange(8 * pair_count, dtype=jnp.int32)[:, None]
    block = 2 * (place % pair_count) + place // (2 * pair_count) % 2
    side_b = place // pair_count % 2 == 1
    parity = jnp.arange(aux_count * 2 * SLOTS, dtype=jnp.int32)[None, :] // SLOTS % 2
    hit = jnp.where(side_b, spread(cols_b) == block, spread(cols_a) == block)
    pick = jnp.where(hit & (parity == place // (4 * pair_count)), -1.0, 0.0).astype(jnp.bfloat16)

    blocks = pl.pallas_call(
        term_kernel,
        out_shape=jax.ShapeDtypeStruct((width * SLOTS, LANES), jnp.bfloat16),
        in_specs=[smem, vmem, vmem, vmem],
        out_specs=vmem,
        scratch_shapes=[pltpu.VMEM((width * SLOTS, LANES), jnp.float32)],
        compiler_params=pltpu.CompilerParams(vmem_limit_bytes=TERM_LIMIT),
        name="term",
    )(owner.reshape(item_count), late, early, metric_tiles)
    rows = width // aux_count
    blocks, pick = lax.optimization_barrier((blocks, pick))
    parts = lax.all_to_all(
        blocks.reshape(aux_count, rows * SLOTS, LANES), "aux", split_axis=0, concat_axis=0, tiled=True
    )

    sums = pl.pallas_call(
        combine_kernel,
        out_shape=jax.ShapeDtypeStruct((pair_count * rows, LANES), jnp.float32),
        in_specs=[vmem] * 2,
        out_specs=vmem,
        compiler_params=small,
        name="combine",
    )(parts, pick)
    arrived = lax.all_to_all(
        sums.reshape(pair_count, rows, LANES), "pair", split_axis=0, concat_axis=0, tiled=True
    )
    return pl.pallas_call(
        final_kernel,
        out_shape=jax.ShapeDtypeStruct((2, rows, width), jnp.float32),
        in_specs=[vmem],
        out_specs=vmem,
        compiler_params=small,
        name="final",
    )(arrived)


def solution(mesh):
    return jax.shard_map(
        shards,
        mesh=mesh,
        in_specs=(
            P(("pair", "aux"), None, None),
            P("pair", None),
            P("pair", None),
            P(("pair", "aux")),
            P(("pair", "aux")),
            P(("pair", "aux"), None),
            P(("pair", "aux")),
            P("aux", None, None),
        ),
        out_specs=P("pair", "aux", None),
        check_vma=False,
    )
```

```python
import jax
import jax.numpy as jnp
from jax import lax
from jax.experimental import pallas as pl
from jax.experimental.pallas import tpu as pltpu
from jax.sharding import PartitionSpec as P

LANES = 128
HALF = 64
MIB = 1 << 20
EARLY_LIMIT = 55_200_000
SERVE_LIMIT = 8 * MIB
LATE_LIMIT = 51_000_000
TERM_LIMIT = 51_000_000
SLOTS = 8


def request_kernel(owner_ref, local_ref, col_ref, out_ref):
    aux_count = out_ref.shape[0]
    shape = (aux_count, owner_ref.shape[1])
    position = lax.broadcasted_iota(jnp.int32, shape, 1)
    match = owner_ref[...] == lax.broadcasted_iota(jnp.int32, shape, 0)
    local = jnp.broadcast_to(local_ref[...], shape)
    first = jnp.min(jnp.where(match, position, LANES), axis=1, keepdims=True)
    last = jnp.max(jnp.where(match, position, -1), axis=1, keepdims=True)
    out_ref[...] = jnp.zeros_like(out_ref)
    out_ref[:, 0:1] = jnp.sum(jnp.where(position == first, local, 0), axis=1, keepdims=True)
    out_ref[:, 1:2] = jnp.sum(jnp.where(position == last, local, 0), axis=1, keepdims=True)
    out_ref[:, 32 : 32 + shape[1]] = jnp.broadcast_to(col_ref[...], shape)


def place(metric_ref, coeff_ref, support_ref, padded_ref, picked_ref, rows_ref):
    aux_width, blocks, _ = metric_ref.shape
    width = coeff_ref.shape[0] // support_ref.shape[0]
    shape = (coeff_ref.shape[1], support_ref.shape[1])
    for block in range(support_ref.shape[0]):
        onehot = support_ref[block : block + 1, :] == lax.broadcasted_iota(jnp.int32, shape, 0)
        chosen = jnp.dot(
            coeff_ref[block * width : (block + 1) * width, :],
            onehot.astype(jnp.float32).astype(jnp.bfloat16),
            preferred_element_type=jnp.float32,
        )
        picked_ref[block] = chosen.T.astype(jnp.bfloat16)
    rows_ref[...] = jnp.zeros_like(rows_ref)
    for p in range(aux_width):
        rows_ref[p * blocks : (p + 1) * blocks, :aux_width] = metric_ref[p].astype(jnp.float32)
    padded_ref[...] = jnp.zeros_like(padded_ref)
    for block in range(blocks):
        entry = rows_ref[pl.ds(block, aux_width, stride=blocks), :]
        padded_ref[block, :aux_width, :] = (entry + pltpu.roll(entry, HALF, 1)).astype(jnp.bfloat16)


def fetch(tile_ref, first, buffer_ref, sems):
    copies = [
        pltpu.make_async_copy(tile_ref.at[first + item], buffer_ref.at[item], sems.at[item])
        for item in range(buffer_ref.shape[0])
    ]
    for copy in copies:
        copy.start()
    return copies


def half_tiles(row_ref, first, picked_ref, copies, buffer_ref, half_ref, slab_ref, put):
    item_count, width, columns = buffer_ref.shape
    orbitals = picked_ref.shape[1]
    groups = orbitals // 2
    aux_width = columns // width
    lane = lax.broadcasted_iota(jnp.int32, (orbitals, LANES), 1)
    low = lane[:groups] < HALF

    def multiply(item):
        copies[item].wait()
        half_ref[item % 2] = jnp.dot(
            picked_ref[row_ref[first + item]], buffer_ref[item], preferred_element_type=jnp.float32
        )

    multiply(0)
    for item in range(item_count):
        if item + 1 < item_count:
            multiply(item + 1)
        half, slabs = half_ref.at[item % 2], slab_ref.at[item % 2]
        for nu in range(width):
            start = nu * aux_width
            base, shift = start // LANES * LANES, start % LANES
            window = half[:, base : base + LANES]
            if shift + aux_width > LANES:
                window = jnp.where(lane >= shift, window, half[:, base + LANES : base + 2 * LANES])
            front, back = window[:groups], window[groups:]
            if shift:
                front = pltpu.roll(front, LANES - shift, 1)
            if shift != HALF:
                back = pltpu.roll(back, (LANES + HALF - shift) % LANES, 1)
            slabs[nu * groups : (nu + 1) * groups, :] = jnp.where(low, front, back)
        for g in range(groups):
            put(item, g * width, slabs[pl.ds(g, width, stride=groups), :].astype(jnp.bfloat16))


def early_kernel(row_ref, tile_ref, metric_ref, coeff_ref, support_ref, *refs):
    out_ref, padded_ref, picked_ref, rows_ref, made_ref, buffer_ref, half_ref, slab_ref, sems = refs
    count = buffer_ref.shape[0]
    first = tile_ref.shape[0] - count
    copies = fetch(tile_ref, first, buffer_ref, sems)
    place(metric_ref, coeff_ref, support_ref, padded_ref, picked_ref, rows_ref)
    sends = [
        pltpu.make_async_copy(made_ref.at[item], out_ref.at[item], sems.at[count + item])
        for item in range(count)
    ]

    def put(item, at, rows):
        made_ref[item, at : at + rows.shape[0], :] = rows
        if at + rows.shape[0] == made_ref.shape[1]:
            sends[item].start()

    half_tiles(row_ref, first, picked_ref, copies, buffer_ref, half_ref, slab_ref, put)
    for send in sends:
        send.wait()


def late_kernel(row_ref, tile_ref, picked_ref, out_ref, buffer_ref, half_ref, slab_ref, sems):
    copies = fetch(tile_ref, 0, buffer_ref, sems)

    def put(item, at, rows):
        out_ref[item, at : at + rows.shape[0], :] = rows

    half_tiles(row_ref, 0, picked_ref, copies, buffer_ref, half_ref, slab_ref, put)


def serve_kernel(asked_ref, metric_ref, out_ref):
    lane = lax.broadcasted_iota(jnp.int32, out_ref.shape[1:], 1)
    for peer in range(out_ref.shape[0]):
        out_ref[peer] = jnp.where(
            lane < HALF, metric_ref[asked_ref[peer, 0]], metric_ref[asked_ref[peer, 1]]
        )


def term_kernel(owner_ref, late_ref, early_ref, metric_ref, out_ref, total):
    late_count, rows, _ = late_ref.shape
    item_count = late_count + early_ref.shape[0]
    width = out_ref.shape[0] // SLOTS
    depth = metric_ref.shape[1]
    steps = (item_count + 1) // 2
    gap = item_count - steps
    groups = rows // width
    lane = lax.broadcasted_iota(jnp.int32, (depth, LANES), 1)
    rest = jnp.zeros((HALF - depth, LANES), jnp.float32)

    def placed(item):
        mine = owner_ref[item]
        slot = jnp.int32(0)
        for other in range(item):
            slot = slot | jnp.where(owner_ref[other] == mine, 1, 0)
        block = metric_ref[mine].astype(jnp.float32)
        turned = pltpu.roll(block, HALF, 1)
        low = jnp.where(slot == 0, block, turned)
        high = jnp.where(slot == 0, turned, block)
        stacked = [jnp.where(lane < HALF, low, 0.0), rest, jnp.where(lane < HALF, 0.0, high), rest]
        return jnp.concatenate(stacked, axis=0).astype(jnp.bfloat16)

    def spread(array):
        return jnp.concatenate(
            [array[g * width : (g + 1) * width, :] for g in range(groups)], axis=1
        )

    def term(item):
        halves = late_ref[item] if item < late_count else early_ref[item - late_count]
        fitted = jnp.dot(halves, placed(item), preferred_element_type=jnp.float32)
        return lax.dot_general(
            spread(halves),
            spread(fitted.astype(jnp.bfloat16)),
            (((1,), (1,)), ((), ())),
            preferred_element_type=jnp.float32,
        )

    total[...] = jnp.zeros_like(total)
    terms = []
    for item in range(item_count):
        terms.append(term(item))
        if item >= gap and item - gap < steps:
            at = item - gap
            total[pl.ds(at, width, stride=SLOTS), :] = jnp.concatenate(
                [terms[at], terms[item]], axis=1
            )
    out_ref[...] = total[...].astype(jnp.bfloat16)


def combine_kernel(parts_ref, pick_ref, out_ref):
    sources = parts_ref.shape[0]
    rows = parts_ref.shape[1] // SLOTS
    pairs = pick_ref.shape[0] // 8
    low = lax.broadcasted_iota(jnp.int32, (pairs, LANES), 1) < HALF
    for step in range(rows // 2):
        block = parts_ref[:, step * 2 * SLOTS : (step + 1) * 2 * SLOTS, :]
        summed = jnp.dot(
            pick_ref[...],
            block.reshape(sources * 2 * SLOTS, LANES),
            preferred_element_type=jnp.float32,
        )
        for parity in range(2):
            at = parity * 4 * pairs
            even = summed[at : at + pairs] + pltpu.roll(summed[at + pairs : at + 2 * pairs], HALF, 1)
            odd = summed[at + 3 * pairs : at + 4 * pairs] + pltpu.roll(
                summed[at + 2 * pairs : at + 3 * pairs], HALF, 1
            )
            out_ref[pl.ds(step * 2 + parity, pairs, stride=rows), :] = jnp.where(low, even, odd)


def final_kernel(parts_ref, out_ref):
    rows = out_ref.shape[1]
    summed = jnp.sum(parts_ref[...], axis=0)
    for side in range(out_ref.shape[0]):
        out_ref[side] = summed[:, side * HALF : (side + 1) * HALF]


def shards(tiles, coeff, support, row_block, col_block, owner, local_block, metric):
    item_count, width, columns = tiles.shape
    aux_width = metric.shape[1]
    orbitals = support.shape[1]
    aux_count = lax.axis_size("aux")
    pair_count = lax.axis_size("pair")
    groups = orbitals // 2
    pair_steps = (item_count + 1) // 2
    gap = item_count - pair_steps
    vmem = pl.BlockSpec(memory_space=pltpu.VMEM)
    smem = pl.BlockSpec(memory_space=pltpu.SMEM)
    anywhere = pl.BlockSpec(memory_space=pl.ANY)
    small = pltpu.CompilerParams(vmem_limit_bytes=8 * MIB)
    row = lambda array: array.reshape(1, item_count)

    request = pl.pallas_call(
        request_kernel,
        out_shape=jax.ShapeDtypeStruct((aux_count, LANES), jnp.int32),
        in_specs=[vmem] * 3,
        out_specs=vmem,
        name="request",
    )(row(owner), row(local_block), row(col_block))
    asked = lax.all_to_all(
        request.reshape(aux_count, 1, LANES), "aux", split_axis=0, concat_axis=0, tiled=True
    ).reshape(aux_count, LANES)

    late_rows = groups * width
    by_aux = metric.transpose(1, 0, 2)
    depth = -(-aux_width // 8) * 8
    early_count = item_count * 3 // 11
    late_count = item_count - early_count

    def half_scratch(count):
        return [
            pltpu.VMEM((count, width, columns), jnp.bfloat16),
            pltpu.VMEM((2, orbitals, columns), jnp.float32),
            pltpu.VMEM((2, late_rows, LANES), jnp.float32),
            pltpu.SemaphoreType.DMA((2 * count,)),
        ]

    def cost(count):
        return pl.CostEstimate(
            flops=2 * count * orbitals * width * columns,
            bytes_accessed=2 * count * (width * columns + late_rows * LANES),
            transcendentals=0,
        )

    early, padded, picked = pl.pallas_call(
        early_kernel,
        out_shape=[
            jax.ShapeDtypeStruct((early_count, late_rows, LANES), jnp.bfloat16),
            jax.ShapeDtypeStruct((metric.shape[0], depth, LANES), jnp.bfloat16),
            jax.ShapeDtypeStruct((support.shape[0], orbitals, width), jnp.bfloat16),
        ],
        in_specs=[smem, anywhere, vmem, vmem, vmem],
        out_specs=[anywhere, vmem, vmem],
        scratch_shapes=[
            pltpu.VMEM((aux_width * metric.shape[0], LANES), jnp.float32),
            pltpu.VMEM((early_count, late_rows, LANES), jnp.bfloat16),
        ]
        + half_scratch(early_count),
        compiler_params=pltpu.CompilerParams(vmem_limit_bytes=EARLY_LIMIT),
        cost_estimate=cost(early_count),
        name="early",
    )(row_block, tiles, by_aux, coeff, support)

    served = pl.pallas_call(
        serve_kernel,
        out_shape=jax.ShapeDtypeStruct((aux_count, depth, LANES), jnp.bfloat16),
        in_specs=[smem, vmem],
        out_specs=vmem,
        compiler_params=pltpu.CompilerParams(vmem_limit_bytes=SERVE_LIMIT),
        name="serve",
    )(asked, padded)
    metric_tiles = lax.all_to_all(served, "aux", split_axis=0, concat_axis=0, tiled=True)

    picked, _ = lax.optimization_barrier((picked, served))
    late = pl.pallas_call(
        late_kernel,
        out_shape=jax.ShapeDtypeStruct((late_count, late_rows, LANES), jnp.bfloat16),
        in_specs=[smem, anywhere, vmem],
        out_specs=vmem,
        scratch_shapes=half_scratch(late_count),
        compiler_params=pltpu.CompilerParams(vmem_limit_bytes=LATE_LIMIT),
        cost_estimate=cost(late_count),
        name="late",
    )(row_block, tiles, picked)

    cols = asked[:, 32 : 32 + item_count]
    fill = ((0, 0), (0, SLOTS - pair_steps))
    cols_a = jnp.pad(cols[:, :pair_steps], fill, constant_values=-1)
    cols_b = jnp.pad(cols[:, gap:], fill, constant_values=-1)
    cols_b = jnp.where(jnp.arange(SLOTS)[None, :] < pair_steps - gap, -1, cols_b)
    spread = lambda array: jnp.broadcast_to(array[:, None, :], (aux_count, 2, SLOTS)).reshape(1, -1)
    place = jnp.arange(8 * pair_count, dtype=jnp.int32)[:, None]
    block = 2 * (place % pair_count) + place // (2 * pair_count) % 2
    side_b = place // pair_count % 2 == 1
    parity = jnp.arange(aux_count * 2 * SLOTS, dtype=jnp.int32)[None, :] // SLOTS % 2
    hit = jnp.where(side_b, spread(cols_b) == block, spread(cols_a) == block)
    pick = jnp.where(hit & (parity == place // (4 * pair_count)), -1.0, 0.0).astype(jnp.bfloat16)

    blocks = pl.pallas_call(
        term_kernel,
        out_shape=jax.ShapeDtypeStruct((width * SLOTS, LANES), jnp.bfloat16),
        in_specs=[smem, vmem, vmem, vmem],
        out_specs=vmem,
        scratch_shapes=[pltpu.VMEM((width * SLOTS, LANES), jnp.float32)],
        compiler_params=pltpu.CompilerParams(vmem_limit_bytes=TERM_LIMIT),
        name="term",
    )(owner.reshape(item_count), late, early, metric_tiles)
    rows = width // aux_count
    blocks, pick = lax.optimization_barrier((blocks, pick))
    parts = lax.all_to_all(
        blocks.reshape(aux_count, rows * SLOTS, LANES), "aux", split_axis=0, concat_axis=0, tiled=True
    )

    sums = pl.pallas_call(
        combine_kernel,
        out_shape=jax.ShapeDtypeStruct((pair_count * rows, LANES), jnp.float32),
        in_specs=[vmem] * 2,
        out_specs=vmem,
        compiler_params=small,
        name="combine",
    )(parts, pick)
    arrived = lax.all_to_all(
        sums.reshape(pair_count, rows, LANES), "pair", split_axis=0, concat_axis=0, tiled=True
    )
    return pl.pallas_call(
        final_kernel,
        out_shape=jax.ShapeDtypeStruct((2, rows, width), jnp.float32),
        in_specs=[vmem],
        out_specs=vmem,
        compiler_params=small,
        name="final",
    )(arrived)


def solution(mesh):
    return jax.shard_map(
        shards,
        mesh=mesh,
        in_specs=(
            P(("pair", "aux"), None, None),
            P("pair", None),
            P("pair", None),
            P(("pair", "aux")),
            P(("pair", "aux")),
            P(("pair", "aux"), None),
            P(("pair", "aux")),
            P("aux", None, None),
        ),
        out_specs=P("pair", "aux", None),
        check_vma=False,
    )
```

```python
import jax
import jax.numpy as jnp
from jax import lax
from jax.experimental import pallas as pl
from jax.experimental.pallas import tpu as pltpu
from jax.sharding import PartitionSpec as P

LANES = 128
HALF = 64
MIB = 1 << 20
EARLY_ROOM = 40
EARLY_LIMIT = 55_200_000
SERVE_LIMIT = 8 * MIB
LATE_LIMIT = 51_000_000
TERM_LIMIT = 51_000_000
SLOTS = 8


def request_kernel(owner_ref, local_ref, col_ref, out_ref):
    aux_count = out_ref.shape[0]
    shape = (aux_count, owner_ref.shape[1])
    position = lax.broadcasted_iota(jnp.int32, shape, 1)
    match = owner_ref[...] == lax.broadcasted_iota(jnp.int32, shape, 0)
    local = jnp.broadcast_to(local_ref[...], shape)
    first = jnp.min(jnp.where(match, position, LANES), axis=1, keepdims=True)
    last = jnp.max(jnp.where(match, position, -1), axis=1, keepdims=True)
    out_ref[...] = jnp.zeros_like(out_ref)
    out_ref[:, 0:1] = jnp.sum(jnp.where(position == first, local, 0), axis=1, keepdims=True)
    out_ref[:, 1:2] = jnp.sum(jnp.where(position == last, local, 0), axis=1, keepdims=True)
    out_ref[:, 32 : 32 + shape[1]] = jnp.broadcast_to(col_ref[...], shape)


def place(metric_ref, coeff_ref, support_ref, padded_ref, picked_ref, rows_ref):
    aux_width, blocks, _ = metric_ref.shape
    width = coeff_ref.shape[0] // support_ref.shape[0]
    shape = (coeff_ref.shape[1], support_ref.shape[1])
    for block in range(support_ref.shape[0]):
        onehot = support_ref[block : block + 1, :] == lax.broadcasted_iota(jnp.int32, shape, 0)
        chosen = jnp.dot(
            coeff_ref[block * width : (block + 1) * width, :],
            onehot.astype(jnp.float32).astype(jnp.bfloat16),
            preferred_element_type=jnp.float32,
        )
        picked_ref[block] = chosen.T.astype(jnp.bfloat16)
    rows_ref[...] = jnp.zeros_like(rows_ref)
    for p in range(aux_width):
        rows_ref[p * blocks : (p + 1) * blocks, :aux_width] = metric_ref[p].astype(jnp.float32)
    padded_ref[...] = jnp.zeros_like(padded_ref)
    for block in range(blocks):
        entry = rows_ref[pl.ds(block, aux_width, stride=blocks), :]
        padded_ref[block, :aux_width, :] = (entry + pltpu.roll(entry, HALF, 1)).astype(jnp.bfloat16)


def fetch(tile_ref, first, buffer_ref, sems):
    copies = [
        pltpu.make_async_copy(tile_ref.at[first + item], buffer_ref.at[item], sems.at[item])
        for item in range(buffer_ref.shape[0])
    ]
    for copy in copies:
        copy.start()
    return copies


def half_tiles(row_ref, first, picked_ref, copies, buffer_ref, half_ref, slab_ref, put):
    item_count, width, columns = buffer_ref.shape
    orbitals = picked_ref.shape[1]
    groups = orbitals // 2
    aux_width = columns // width
    lane = lax.broadcasted_iota(jnp.int32, (orbitals, LANES), 1)
    low = lane[:groups] < HALF

    def multiply(item):
        copies[item].wait()
        half_ref[item % 2] = jnp.dot(
            picked_ref[row_ref[first + item]], buffer_ref[item], preferred_element_type=jnp.float32
        )

    multiply(0)
    for item in range(item_count):
        if item + 1 < item_count:
            multiply(item + 1)
        half, slabs = half_ref.at[item % 2], slab_ref.at[item % 2]
        for nu in range(width):
            start = nu * aux_width
            base, shift = start // LANES * LANES, start % LANES
            window = half[:, base : base + LANES]
            if shift + aux_width > LANES:
                window = jnp.where(lane >= shift, window, half[:, base + LANES : base + 2 * LANES])
            front, back = window[:groups], window[groups:]
            if shift:
                front = pltpu.roll(front, LANES - shift, 1)
            if shift != HALF:
                back = pltpu.roll(back, (LANES + HALF - shift) % LANES, 1)
            slabs[nu * groups : (nu + 1) * groups, :] = jnp.where(low, front, back)
        for g in range(groups):
            put(item, g * width, slabs[pl.ds(g, width, stride=groups), :].astype(jnp.bfloat16))


def early_kernel(row_ref, tile_ref, metric_ref, coeff_ref, support_ref, *refs):
    out_ref, padded_ref, picked_ref, rows_ref, made_ref, buffer_ref, half_ref, slab_ref, sems = refs
    count = buffer_ref.shape[0]
    first = tile_ref.shape[0] - count
    copies = fetch(tile_ref, first, buffer_ref, sems)
    place(metric_ref, coeff_ref, support_ref, padded_ref, picked_ref, rows_ref)
    sends = [
        pltpu.make_async_copy(made_ref.at[item], out_ref.at[item], sems.at[count + item])
        for item in range(count)
    ]

    def put(item, at, rows):
        made_ref[item, at : at + rows.shape[0], :] = rows
        if at + rows.shape[0] == made_ref.shape[1]:
            sends[item].start()

    half_tiles(row_ref, first, picked_ref, copies, buffer_ref, half_ref, slab_ref, put)
    for send in sends:
        send.wait()


def late_kernel(row_ref, tile_ref, picked_ref, out_ref, buffer_ref, half_ref, slab_ref, sems):
    copies = fetch(tile_ref, 0, buffer_ref, sems)

    def put(item, at, rows):
        out_ref[item, at : at + rows.shape[0], :] = rows

    half_tiles(row_ref, 0, picked_ref, copies, buffer_ref, half_ref, slab_ref, put)


def serve_kernel(asked_ref, metric_ref, out_ref):
    lane = lax.broadcasted_iota(jnp.int32, out_ref.shape[1:], 1)
    for peer in range(out_ref.shape[0]):
        out_ref[peer] = jnp.where(
            lane < HALF, metric_ref[asked_ref[peer, 0]], metric_ref[asked_ref[peer, 1]]
        )


def term_kernel(owner_ref, late_ref, early_ref, metric_ref, out_ref, buffer_ref, total, sems):
    late_count, rows, _ = late_ref.shape
    item_count = late_count + buffer_ref.shape[0]
    copies = fetch(early_ref, 0, buffer_ref, sems)
    width = out_ref.shape[0] // SLOTS
    depth = metric_ref.shape[1]
    steps = (item_count + 1) // 2
    gap = item_count - steps
    groups = rows // width
    lane = lax.broadcasted_iota(jnp.int32, (depth, LANES), 1)
    rest = jnp.zeros((HALF - depth, LANES), jnp.float32)

    def placed(item):
        mine = owner_ref[item]
        slot = jnp.int32(0)
        for other in range(item):
            slot = slot | jnp.where(owner_ref[other] == mine, 1, 0)
        block = metric_ref[mine].astype(jnp.float32)
        turned = pltpu.roll(block, HALF, 1)
        low = jnp.where(slot == 0, block, turned)
        high = jnp.where(slot == 0, turned, block)
        stacked = [jnp.where(lane < HALF, low, 0.0), rest, jnp.where(lane < HALF, 0.0, high), rest]
        return jnp.concatenate(stacked, axis=0).astype(jnp.bfloat16)

    def spread(array):
        return jnp.concatenate(
            [array[g * width : (g + 1) * width, :] for g in range(groups)], axis=1
        )

    def term(item):
        if item < late_count:
            halves = late_ref[item]
        else:
            copies[item - late_count].wait()
            halves = buffer_ref[item - late_count]
        fitted = jnp.dot(halves, placed(item), preferred_element_type=jnp.float32)
        return lax.dot_general(
            spread(halves),
            spread(fitted.astype(jnp.bfloat16)),
            (((1,), (1,)), ((), ())),
            preferred_element_type=jnp.float32,
        )

    total[...] = jnp.zeros_like(total)
    terms = []
    for item in range(item_count):
        terms.append(term(item))
        if item >= gap and item - gap < steps:
            at = item - gap
            total[pl.ds(at, width, stride=SLOTS), :] = jnp.concatenate(
                [terms[at], terms[item]], axis=1
            )
    out_ref[...] = total[...].astype(jnp.bfloat16)


def combine_kernel(parts_ref, pick_ref, out_ref):
    sources = parts_ref.shape[0]
    rows = parts_ref.shape[1] // SLOTS
    pairs = pick_ref.shape[0] // 8
    low = lax.broadcasted_iota(jnp.int32, (pairs, LANES), 1) < HALF
    for step in range(rows // 2):
        block = parts_ref[:, step * 2 * SLOTS : (step + 1) * 2 * SLOTS, :]
        summed = jnp.dot(
            pick_ref[...],
            block.reshape(sources * 2 * SLOTS, LANES),
            preferred_element_type=jnp.float32,
        )
        for parity in range(2):
            at = parity * 4 * pairs
            even = summed[at : at + pairs] + pltpu.roll(summed[at + pairs : at + 2 * pairs], HALF, 1)
            odd = summed[at + 3 * pairs : at + 4 * pairs] + pltpu.roll(
                summed[at + 2 * pairs : at + 3 * pairs], HALF, 1
            )
            out_ref[pl.ds(step * 2 + parity, pairs, stride=rows), :] = jnp.where(low, even, odd)


def final_kernel(parts_ref, out_ref):
    rows = out_ref.shape[1]
    summed = jnp.sum(parts_ref[...], axis=0)
    for side in range(out_ref.shape[0]):
        out_ref[side] = summed[:, side * HALF : (side + 1) * HALF]


def shards(tiles, coeff, support, row_block, col_block, owner, local_block, metric):
    item_count, width, columns = tiles.shape
    aux_width = metric.shape[1]
    orbitals = support.shape[1]
    aux_count = lax.axis_size("aux")
    pair_count = lax.axis_size("pair")
    groups = orbitals // 2
    pair_steps = (item_count + 1) // 2
    gap = item_count - pair_steps
    vmem = pl.BlockSpec(memory_space=pltpu.VMEM)
    smem = pl.BlockSpec(memory_space=pltpu.SMEM)
    anywhere = pl.BlockSpec(memory_space=pl.ANY)
    small = pltpu.CompilerParams(vmem_limit_bytes=8 * MIB)
    row = lambda array: array.reshape(1, item_count)

    request = pl.pallas_call(
        request_kernel,
        out_shape=jax.ShapeDtypeStruct((aux_count, LANES), jnp.int32),
        in_specs=[vmem] * 3,
        out_specs=vmem,
        name="request",
    )(row(owner), row(local_block), row(col_block))
    asked = lax.all_to_all(
        request.reshape(aux_count, 1, LANES), "aux", split_axis=0, concat_axis=0, tiled=True
    ).reshape(aux_count, LANES)

    late_rows = groups * width
    by_aux = metric.transpose(1, 0, 2)
    depth = -(-aux_width // 8) * 8
    early_count = item_count * 3 // 11
    late_count = item_count - early_count

    def half_scratch(count):
        return [
            pltpu.VMEM((count, width, columns), jnp.bfloat16),
            pltpu.VMEM((2, orbitals, columns), jnp.float32),
            pltpu.VMEM((2, late_rows, LANES), jnp.float32),
            pltpu.SemaphoreType.DMA((2 * count,)),
        ]

    def cost(count):
        return pl.CostEstimate(
            flops=2 * count * orbitals * width * columns,
            bytes_accessed=2 * count * (width * columns + late_rows * LANES),
            transcendentals=0,
        )

    early, padded, picked = pl.pallas_call(
        early_kernel,
        out_shape=[
            jax.ShapeDtypeStruct((EARLY_ROOM, late_rows, LANES), jnp.bfloat16),
            jax.ShapeDtypeStruct((metric.shape[0], depth, LANES), jnp.bfloat16),
            jax.ShapeDtypeStruct((support.shape[0], orbitals, width), jnp.bfloat16),
        ],
        in_specs=[smem, anywhere, vmem, vmem, vmem],
        out_specs=[anywhere, vmem, vmem],
        scratch_shapes=[
            pltpu.VMEM((aux_width * metric.shape[0], LANES), jnp.float32),
            pltpu.VMEM((early_count, late_rows, LANES), jnp.bfloat16),
        ]
        + half_scratch(early_count),
        compiler_params=pltpu.CompilerParams(vmem_limit_bytes=EARLY_LIMIT),
        cost_estimate=cost(early_count),
        name="early",
    )(row_block, tiles, by_aux, coeff, support)

    served = pl.pallas_call(
        serve_kernel,
        out_shape=jax.ShapeDtypeStruct((aux_count, depth, LANES), jnp.bfloat16),
        in_specs=[smem, vmem],
        out_specs=vmem,
        compiler_params=pltpu.CompilerParams(vmem_limit_bytes=SERVE_LIMIT),
        name="serve",
    )(asked, padded)
    metric_tiles = lax.all_to_all(served, "aux", split_axis=0, concat_axis=0, tiled=True)

    picked, _ = lax.optimization_barrier((picked, served))
    late = pl.pallas_call(
        late_kernel,
        out_shape=jax.ShapeDtypeStruct((late_count, late_rows, LANES), jnp.bfloat16),
        in_specs=[smem, anywhere, vmem],
        out_specs=vmem,
        scratch_shapes=half_scratch(late_count),
        compiler_params=pltpu.CompilerParams(vmem_limit_bytes=LATE_LIMIT),
        cost_estimate=cost(late_count),
        name="late",
    )(row_block, tiles, picked)

    cols = asked[:, 32 : 32 + item_count]
    fill = ((0, 0), (0, SLOTS - pair_steps))
    cols_a = jnp.pad(cols[:, :pair_steps], fill, constant_values=-1)
    cols_b = jnp.pad(cols[:, gap:], fill, constant_values=-1)
    cols_b = jnp.where(jnp.arange(SLOTS)[None, :] < pair_steps - gap, -1, cols_b)
    spread = lambda array: jnp.broadcast_to(array[:, None, :], (aux_count, 2, SLOTS)).reshape(1, -1)
    place = jnp.arange(8 * pair_count, dtype=jnp.int32)[:, None]
    block = 2 * (place % pair_count) + place // (2 * pair_count) % 2
    side_b = place // pair_count % 2 == 1
    parity = jnp.arange(aux_count * 2 * SLOTS, dtype=jnp.int32)[None, :] // SLOTS % 2
    hit = jnp.where(side_b, spread(cols_b) == block, spread(cols_a) == block)
    pick = jnp.where(hit & (parity == place // (4 * pair_count)), -1.0, 0.0).astype(jnp.bfloat16)

    blocks = pl.pallas_call(
        term_kernel,
        out_shape=jax.ShapeDtypeStruct((width * SLOTS, LANES), jnp.bfloat16),
        in_specs=[smem, vmem, anywhere, vmem],
        out_specs=vmem,
        scratch_shapes=[
            pltpu.VMEM((early_count, late_rows, LANES), jnp.bfloat16),
            pltpu.VMEM((width * SLOTS, LANES), jnp.float32),
            pltpu.SemaphoreType.DMA((early_count,)),
        ],
        compiler_params=pltpu.CompilerParams(vmem_limit_bytes=TERM_LIMIT),
        name="term",
    )(owner.reshape(item_count), late, early, metric_tiles)
    rows = width // aux_count
    blocks, pick = lax.optimization_barrier((blocks, pick))
    parts = lax.all_to_all(
        blocks.reshape(aux_count, rows * SLOTS, LANES), "aux", split_axis=0, concat_axis=0, tiled=True
    )

    sums = pl.pallas_call(
        combine_kernel,
        out_shape=jax.ShapeDtypeStruct((pair_count * rows, LANES), jnp.float32),
        in_specs=[vmem] * 2,
        out_specs=vmem,
        compiler_params=small,
        name="combine",
    )(parts, pick)
    arrived = lax.all_to_all(
        sums.reshape(pair_count, rows, LANES), "pair", split_axis=0, concat_axis=0, tiled=True
    )
    return pl.pallas_call(
        final_kernel,
        out_shape=jax.ShapeDtypeStruct((2, rows, width), jnp.float32),
        in_specs=[vmem],
        out_specs=vmem,
        compiler_params=small,
        name="final",
    )(arrived)


def solution(mesh):
    return jax.shard_map(
        shards,
        mesh=mesh,
        in_specs=(
            P(("pair", "aux"), None, None),
            P("pair", None),
            P("pair", None),
            P(("pair", "aux")),
            P(("pair", "aux")),
            P(("pair", "aux"), None),
            P(("pair", "aux")),
            P("aux", None, None),
        ),
        out_specs=P("pair", "aux", None),
        check_vma=False,
    )
```

```python
import functools
import jax
import jax.numpy as jnp
from jax import lax
from jax.experimental import pallas as pl
from jax.experimental.pallas import tpu as pltpu
from jax.sharding import PartitionSpec as P

LANES = 128
HALF = 64
MIB = 1 << 20
EARLY_LIMIT = 55_200_000
SERVE_LIMIT = 8 * MIB
LATE_LIMIT = 51_000_000
TERM_LIMIT = 51_000_000
SLOTS = 8


def request_kernel(owner_ref, local_ref, col_ref, out_ref):
    aux_count = out_ref.shape[0]
    shape = (aux_count, owner_ref.shape[1])
    position = lax.broadcasted_iota(jnp.int32, shape, 1)
    match = owner_ref[...] == lax.broadcasted_iota(jnp.int32, shape, 0)
    local = jnp.broadcast_to(local_ref[...], shape)
    first = jnp.min(jnp.where(match, position, LANES), axis=1, keepdims=True)
    last = jnp.max(jnp.where(match, position, -1), axis=1, keepdims=True)
    out_ref[...] = jnp.zeros_like(out_ref)
    out_ref[:, 0:1] = jnp.sum(jnp.where(position == first, local, 0), axis=1, keepdims=True)
    out_ref[:, 1:2] = jnp.sum(jnp.where(position == last, local, 0), axis=1, keepdims=True)
    out_ref[:, 32 : 32 + shape[1]] = jnp.broadcast_to(col_ref[...], shape)


def place(metric_ref, coeff_ref, support_ref, padded_ref, picked_ref, rows_ref):
    aux_width, blocks, _ = metric_ref.shape
    width = coeff_ref.shape[0] // support_ref.shape[0]
    shape = (coeff_ref.shape[1], support_ref.shape[1])
    for block in range(support_ref.shape[0]):
        onehot = support_ref[block : block + 1, :] == lax.broadcasted_iota(jnp.int32, shape, 0)
        chosen = jnp.dot(
            coeff_ref[block * width : (block + 1) * width, :],
            onehot.astype(jnp.float32).astype(jnp.bfloat16),
            preferred_element_type=jnp.float32,
        )
        picked_ref[block] = chosen.T.astype(jnp.bfloat16)
    rows_ref[...] = jnp.zeros_like(rows_ref)
    for p in range(aux_width):
        rows_ref[p * blocks : (p + 1) * blocks, :aux_width] = metric_ref[p].astype(jnp.float32)
    padded_ref[...] = jnp.zeros_like(padded_ref)
    for block in range(blocks):
        entry = rows_ref[pl.ds(block, aux_width, stride=blocks), :]
        padded_ref[block, :aux_width, :] = (entry + pltpu.roll(entry, HALF, 1)).astype(jnp.bfloat16)


def fetch(tile_ref, first, buffer_ref, sems):
    copies = [
        pltpu.make_async_copy(tile_ref.at[first + item], buffer_ref.at[item], sems.at[item])
        for item in range(buffer_ref.shape[0])
    ]
    for copy in copies:
        copy.start()
    return copies


def half_tiles(row_ref, first, picked_ref, copies, buffer_ref, half_ref, slab_ref, put):
    item_count, width, columns = buffer_ref.shape
    orbitals = picked_ref.shape[1]
    groups = orbitals // 2
    aux_width = columns // width
    lane = lax.broadcasted_iota(jnp.int32, (orbitals, LANES), 1)
    low = lane[:groups] < HALF

    def multiply(item):
        copies[item].wait()
        half_ref[item % 2] = jnp.dot(
            picked_ref[row_ref[first + item]], buffer_ref[item], preferred_element_type=jnp.float32
        )

    multiply(0)
    for item in range(item_count):
        if item + 1 < item_count:
            multiply(item + 1)
        half, slabs = half_ref.at[item % 2], slab_ref.at[item % 2]
        for nu in range(width):
            start = nu * aux_width
            base, shift = start // LANES * LANES, start % LANES
            window = half[:, base : base + LANES]
            if shift + aux_width > LANES:
                window = jnp.where(lane >= shift, window, half[:, base + LANES : base + 2 * LANES])
            front, back = window[:groups], window[groups:]
            if shift:
                front = pltpu.roll(front, LANES - shift, 1)
            if shift != HALF:
                back = pltpu.roll(back, (LANES + HALF - shift) % LANES, 1)
            slabs[nu * groups : (nu + 1) * groups, :] = jnp.where(low, front, back)
        for g in range(groups):
            put(item, g * width, slabs[pl.ds(g, width, stride=groups), :].astype(jnp.bfloat16))


def early_kernel(row_ref, tile_ref, metric_ref, coeff_ref, support_ref, *refs):
    out_ref, padded_ref, picked_ref, rows_ref, made_ref, buffer_ref, half_ref, slab_ref, sems = refs
    count = buffer_ref.shape[0]
    first = tile_ref.shape[0] - count
    copies = fetch(tile_ref, first, buffer_ref, sems)
    place(metric_ref, coeff_ref, support_ref, padded_ref, picked_ref, rows_ref)
    sends = [
        pltpu.make_async_copy(made_ref.at[item], out_ref.at[item], sems.at[count + item])
        for item in range(count)
    ]

    def put(item, at, rows):
        made_ref[item, at : at + rows.shape[0], :] = rows
        if at + rows.shape[0] == made_ref.shape[1]:
            sends[item].start()

    half_tiles(row_ref, first, picked_ref, copies, buffer_ref, half_ref, slab_ref, put)
    for send in sends:
        send.wait()


def late_kernel(row_ref, tile_ref, picked_ref, out_ref, buffer_ref, half_ref, slab_ref, sems):
    copies = fetch(tile_ref, 0, buffer_ref, sems)

    def put(item, at, rows):
        out_ref[item, at : at + rows.shape[0], :] = rows

    half_tiles(row_ref, 0, picked_ref, copies, buffer_ref, half_ref, slab_ref, put)


def serve_kernel(asked_ref, metric_ref, out_ref):
    lane = lax.broadcasted_iota(jnp.int32, out_ref.shape[1:], 1)
    for peer in range(out_ref.shape[0]):
        out_ref[peer] = jnp.where(
            lane < HALF, metric_ref[asked_ref[peer, 0]], metric_ref[asked_ref[peer, 1]]
        )


def term_kernel(first, first_slot, owner_ref, halves_ref, metric_ref, *refs):
    *before, out_ref, total = refs
    item_count, rows, _ = halves_ref.shape
    width = total.shape[0] // SLOTS
    depth = metric_ref.shape[1]
    steps = (item_count + 1) // 2
    groups = rows // width
    lane = lax.broadcasted_iota(jnp.int32, (depth, LANES), 1)
    rest = jnp.zeros((HALF - depth, LANES), jnp.float32)

    def placed(item):
        mine = owner_ref[item]
        slot = jnp.int32(0)
        for other in range(item):
            slot = slot | jnp.where(owner_ref[other] == mine, 1, 0)
        block = metric_ref[mine].astype(jnp.float32)
        turned = pltpu.roll(block, HALF, 1)
        low = jnp.where(slot == 0, block, turned)
        high = jnp.where(slot == 0, turned, block)
        stacked = [jnp.where(lane < HALF, low, 0.0), rest, jnp.where(lane < HALF, 0.0, high), rest]
        return jnp.concatenate(stacked, axis=0).astype(jnp.bfloat16)

    def spread(array):
        return jnp.concatenate(
            [array[g * width : (g + 1) * width, :] for g in range(groups)], axis=1
        )

    def term(item):
        if item >= item_count:
            return jnp.zeros((width, HALF), jnp.float32)
        halves = halves_ref[item]
        fitted = jnp.dot(halves, placed(first + item), preferred_element_type=jnp.float32)
        return lax.dot_general(
            spread(halves),
            spread(fitted.astype(jnp.bfloat16)),
            (((1,), (1,)), ((), ())),
            preferred_element_type=jnp.float32,
        )

    total[...] = before[0][...] if before else jnp.zeros_like(total)
    for step in range(steps):
        total[pl.ds(first_slot + step, width, stride=SLOTS), :] = jnp.concatenate(
            [term(step), term(step + steps)], axis=1
        )
    out_ref[...] = total[...].astype(out_ref.dtype)


def combine_kernel(parts_ref, pick_ref, out_ref):
    sources = parts_ref.shape[0]
    rows = parts_ref.shape[1] // SLOTS
    pairs = pick_ref.shape[0] // 8
    low = lax.broadcasted_iota(jnp.int32, (pairs, LANES), 1) < HALF
    for step in range(rows // 2):
        block = parts_ref[:, step * 2 * SLOTS : (step + 1) * 2 * SLOTS, :]
        summed = jnp.dot(
            pick_ref[...],
            block.reshape(sources * 2 * SLOTS, LANES),
            preferred_element_type=jnp.float32,
        )
        for parity in range(2):
            at = parity * 4 * pairs
            even = summed[at : at + pairs] + pltpu.roll(summed[at + pairs : at + 2 * pairs], HALF, 1)
            odd = summed[at + 3 * pairs : at + 4 * pairs] + pltpu.roll(
                summed[at + 2 * pairs : at + 3 * pairs], HALF, 1
            )
            out_ref[pl.ds(step * 2 + parity, pairs, stride=rows), :] = jnp.where(low, even, odd)


def final_kernel(parts_ref, out_ref):
    rows = out_ref.shape[1]
    summed = jnp.sum(parts_ref[...], axis=0)
    for side in range(out_ref.shape[0]):
        out_ref[side] = summed[:, side * HALF : (side + 1) * HALF]


def shards(tiles, coeff, support, row_block, col_block, owner, local_block, metric):
    item_count, width, columns = tiles.shape
    aux_width = metric.shape[1]
    orbitals = support.shape[1]
    aux_count = lax.axis_size("aux")
    pair_count = lax.axis_size("pair")
    groups = orbitals // 2
    vmem = pl.BlockSpec(memory_space=pltpu.VMEM)
    smem = pl.BlockSpec(memory_space=pltpu.SMEM)
    anywhere = pl.BlockSpec(memory_space=pl.ANY)
    small = pltpu.CompilerParams(vmem_limit_bytes=8 * MIB)
    row = lambda array: array.reshape(1, item_count)

    request = pl.pallas_call(
        request_kernel,
        out_shape=jax.ShapeDtypeStruct((aux_count, LANES), jnp.int32),
        in_specs=[vmem] * 3,
        out_specs=vmem,
        name="request",
    )(row(owner), row(local_block), row(col_block))
    asked = lax.all_to_all(
        request.reshape(aux_count, 1, LANES), "aux", split_axis=0, concat_axis=0, tiled=True
    ).reshape(aux_count, LANES)

    late_rows = groups * width
    by_aux = metric.transpose(1, 0, 2)
    depth = -(-aux_width // 8) * 8
    early_count = item_count * 3 // 11
    late_count = item_count - early_count

    def half_scratch(count):
        return [
            pltpu.VMEM((count, width, columns), jnp.bfloat16),
            pltpu.VMEM((2, orbitals, columns), jnp.float32),
            pltpu.VMEM((2, late_rows, LANES), jnp.float32),
            pltpu.SemaphoreType.DMA((2 * count,)),
        ]

    def cost(count):
        return pl.CostEstimate(
            flops=2 * count * orbitals * width * columns,
            bytes_accessed=2 * count * (width * columns + late_rows * LANES),
            transcendentals=0,
        )

    early, padded, picked = pl.pallas_call(
        early_kernel,
        out_shape=[
            jax.ShapeDtypeStruct((early_count, late_rows, LANES), jnp.bfloat16),
            jax.ShapeDtypeStruct((metric.shape[0], depth, LANES), jnp.bfloat16),
            jax.ShapeDtypeStruct((support.shape[0], orbitals, width), jnp.bfloat16),
        ],
        in_specs=[smem, anywhere, vmem, vmem, vmem],
        out_specs=[anywhere, vmem, vmem],
        scratch_shapes=[
            pltpu.VMEM((aux_width * metric.shape[0], LANES), jnp.float32),
            pltpu.VMEM((early_count, late_rows, LANES), jnp.bfloat16),
        ]
        + half_scratch(early_count),
        compiler_params=pltpu.CompilerParams(vmem_limit_bytes=EARLY_LIMIT),
        cost_estimate=cost(early_count),
        name="early",
    )(row_block, tiles, by_aux, coeff, support)

    served = pl.pallas_call(
        serve_kernel,
        out_shape=jax.ShapeDtypeStruct((aux_count, depth, LANES), jnp.bfloat16),
        in_specs=[smem, vmem],
        out_specs=vmem,
        compiler_params=pltpu.CompilerParams(vmem_limit_bytes=SERVE_LIMIT),
        name="serve",
    )(asked, padded)
    metric_tiles = lax.all_to_all(served, "aux", split_axis=0, concat_axis=0, tiled=True)

    picked, _ = lax.optimization_barrier((picked, served))
    late = pl.pallas_call(
        late_kernel,
        out_shape=jax.ShapeDtypeStruct((late_count, late_rows, LANES), jnp.bfloat16),
        in_specs=[smem, anywhere, vmem],
        out_specs=vmem,
        scratch_shapes=half_scratch(late_count),
        compiler_params=pltpu.CompilerParams(vmem_limit_bytes=LATE_LIMIT),
        cost_estimate=cost(late_count),
        name="late",
    )(row_block, tiles, picked)

    cols = asked[:, 32 : 32 + item_count]
    late_steps, early_steps = (late_count + 1) // 2, (early_count + 1) // 2

    def columns_of(*parts):
        taken = []
        for start, stop, size in parts:
            fill = ((0, 0), (0, size - (stop - start)))
            taken.append(jnp.pad(cols[:, start:stop], fill, constant_values=-1))
        return jnp.concatenate(taken, axis=1)

    spare = SLOTS - late_steps
    cols_a = columns_of(
        (0, late_steps, late_steps), (late_count, late_count + early_steps, spare)
    )
    cols_b = columns_of(
        (late_steps, late_count, late_steps), (late_count + early_steps, item_count, spare)
    )
    spread = lambda array: jnp.broadcast_to(array[:, None, :], (aux_count, 2, SLOTS)).reshape(1, -1)
    place = jnp.arange(8 * pair_count, dtype=jnp.int32)[:, None]
    block = 2 * (place % pair_count) + place // (2 * pair_count) % 2
    side_b = place // pair_count % 2 == 1
    parity = jnp.arange(aux_count * 2 * SLOTS, dtype=jnp.int32)[None, :] // SLOTS % 2
    hit = jnp.where(side_b, spread(cols_b) == block, spread(cols_a) == block)
    pick = jnp.where(hit & (parity == place // (4 * pair_count)), -1.0, 0.0).astype(jnp.bfloat16)

    def terms(first, first_slot, halves, before, dtype, name):
        return pl.pallas_call(
            functools.partial(term_kernel, first, first_slot),
            out_shape=jax.ShapeDtypeStruct((width * SLOTS, LANES), dtype),
            in_specs=[smem] + [vmem] * (2 + len(before)),
            out_specs=vmem,
            scratch_shapes=[pltpu.VMEM((width * SLOTS, LANES), jnp.float32)],
            compiler_params=pltpu.CompilerParams(vmem_limit_bytes=TERM_LIMIT),
            cost_estimate=pl.CostEstimate(
                flops=2 * halves.shape[0] * late_rows * LANES * (LANES + width),
                bytes_accessed=2 * halves.size,
                transcendentals=0,
            ),
            name=name,
        )(owner.reshape(item_count), halves, metric_tiles, *before)

    blocks = terms(0, 0, late, (), jnp.float32, "late_term")
    blocks = terms(late_count, late_steps, early, (blocks,), jnp.bfloat16, "early_term")
    rows = width // aux_count
    blocks, pick = lax.optimization_barrier((blocks, pick))
    parts = lax.all_to_all(
        blocks.reshape(aux_count, rows * SLOTS, LANES), "aux", split_axis=0, concat_axis=0, tiled=True
    )

    sums = pl.pallas_call(
        combine_kernel,
        out_shape=jax.ShapeDtypeStruct((pair_count * rows, LANES), jnp.float32),
        in_specs=[vmem] * 2,
        out_specs=vmem,
        compiler_params=small,
        name="combine",
    )(parts, pick)
    arrived = lax.all_to_all(
        sums.reshape(pair_count, rows, LANES), "pair", split_axis=0, concat_axis=0, tiled=True
    )
    return pl.pallas_call(
        final_kernel,
        out_shape=jax.ShapeDtypeStruct((2, rows, width), jnp.float32),
        in_specs=[vmem],
        out_specs=vmem,
        compiler_params=small,
        name="final",
    )(arrived)


def solution(mesh):
    return jax.shard_map(
        shards,
        mesh=mesh,
        in_specs=(
            P(("pair", "aux"), None, None),
            P("pair", None),
            P("pair", None),
            P(("pair", "aux")),
            P(("pair", "aux")),
            P(("pair", "aux"), None),
            P(("pair", "aux")),
            P("aux", None, None),
        ),
        out_specs=P("pair", "aux", None),
        check_vma=False,
    )
```

```python
import functools
import jax
import jax.numpy as jnp
from jax import lax
from jax.experimental import pallas as pl
from jax.experimental.pallas import tpu as pltpu
from jax.sharding import PartitionSpec as P

LANES = 128
HALF = 64
MIB = 1 << 20
ROOM = 700
EARLY_LIMIT = 61_000_000
SERVE_LIMIT = 51_000_000
LATE_LIMIT = 51_000_000
TERM_LIMIT = 51_000_000
SLOTS = 8


def request_kernel(owner_ref, local_ref, col_ref, out_ref):
    aux_count = out_ref.shape[0]
    shape = (aux_count, owner_ref.shape[1])
    position = lax.broadcasted_iota(jnp.int32, shape, 1)
    match = owner_ref[...] == lax.broadcasted_iota(jnp.int32, shape, 0)
    local = jnp.broadcast_to(local_ref[...], shape)
    first = jnp.min(jnp.where(match, position, LANES), axis=1, keepdims=True)
    last = jnp.max(jnp.where(match, position, -1), axis=1, keepdims=True)
    out_ref[...] = jnp.zeros_like(out_ref)
    out_ref[:, 0:1] = jnp.sum(jnp.where(position == first, local, 0), axis=1, keepdims=True)
    out_ref[:, 1:2] = jnp.sum(jnp.where(position == last, local, 0), axis=1, keepdims=True)
    out_ref[:, 32 : 32 + shape[1]] = jnp.broadcast_to(col_ref[...], shape)


def place(metric_ref, coeff_ref, support_ref, padded_ref, picked_ref, rows_ref):
    aux_width, blocks, _ = metric_ref.shape
    width = coeff_ref.shape[0] // support_ref.shape[0]
    shape = (coeff_ref.shape[1], support_ref.shape[1])
    for block in range(support_ref.shape[0]):
        onehot = support_ref[block : block + 1, :] == lax.broadcasted_iota(jnp.int32, shape, 0)
        chosen = jnp.dot(
            coeff_ref[block * width : (block + 1) * width, :],
            onehot.astype(jnp.float32).astype(jnp.bfloat16),
            preferred_element_type=jnp.float32,
        )
        picked_ref[block] = chosen.T.astype(jnp.bfloat16)
    rows_ref[...] = jnp.zeros_like(rows_ref)
    for p in range(aux_width):
        rows_ref[p * blocks : (p + 1) * blocks, :aux_width] = metric_ref[p].astype(jnp.float32)
    padded_ref[...] = jnp.zeros_like(padded_ref)
    for block in range(blocks):
        entry = rows_ref[pl.ds(block, aux_width, stride=blocks), :]
        padded_ref[block, :aux_width, :] = (entry + pltpu.roll(entry, HALF, 1)).astype(jnp.bfloat16)


def fetch(tile_ref, first, buffer_ref, sems):
    copies = [
        pltpu.make_async_copy(tile_ref.at[first + item], buffer_ref.at[item], sems.at[item])
        for item in range(buffer_ref.shape[0])
    ]
    for copy in copies:
        copy.start()
    return copies


def half_tiles(row_ref, first, picked_ref, copies, buffer_ref, half_ref, slab_ref, put):
    item_count, width, columns = buffer_ref.shape
    orbitals = picked_ref.shape[1]
    groups = orbitals // 2
    aux_width = columns // width
    lane = lax.broadcasted_iota(jnp.int32, (orbitals, LANES), 1)
    low = lane[:groups] < HALF

    def multiply(item):
        copies[item].wait()
        half_ref[item % 2] = jnp.dot(
            picked_ref[row_ref[first + item]], buffer_ref[item], preferred_element_type=jnp.float32
        )

    multiply(0)
    for item in range(item_count):
        if item + 1 < item_count:
            multiply(item + 1)
        half, slabs = half_ref.at[item % 2], slab_ref.at[item % 2]
        for nu in range(width):
            start = nu * aux_width
            base, shift = start // LANES * LANES, start % LANES
            window = half[:, base : base + LANES]
            if shift + aux_width > LANES:
                window = jnp.where(lane >= shift, window, half[:, base + LANES : base + 2 * LANES])
            front, back = window[:groups], window[groups:]
            if shift:
                front = pltpu.roll(front, LANES - shift, 1)
            if shift != HALF:
                back = pltpu.roll(back, (LANES + HALF - shift) % LANES, 1)
            slabs[nu * groups : (nu + 1) * groups, :] = jnp.where(low, front, back)
        for g in range(groups):
            put(item, g * width, slabs[pl.ds(g, width, stride=groups), :].astype(jnp.bfloat16))


def early_kernel(row_ref, tile_ref, metric_ref, coeff_ref, support_ref, *refs):
    out_ref, padded_out, picked_out, padded_ref, picked_ref, rows_ref, made_ref, *refs = refs
    buffer_ref, half_ref, slab_ref, sems = refs
    count = buffer_ref.shape[0]
    first = tile_ref.shape[0] - count
    copies = fetch(tile_ref, first, buffer_ref, sems)
    place(metric_ref, coeff_ref, support_ref, padded_ref, picked_ref, rows_ref)
    placed = [
        pltpu.make_async_copy(ref, out.at[pl.ds(0, ref.shape[0])], sems.at[2 * count + at])
        for at, (ref, out) in enumerate(((padded_ref, padded_out), (picked_ref, picked_out)))
    ]
    for copy in placed:
        copy.start()
    sends = [
        pltpu.make_async_copy(made_ref.at[item], out_ref.at[item], sems.at[count + item])
        for item in range(count)
    ]

    def put(item, at, rows):
        made_ref[item, at : at + rows.shape[0], :] = rows
        if at + rows.shape[0] == made_ref.shape[1]:
            sends[item].start()

    half_tiles(row_ref, first, picked_ref, copies, buffer_ref, half_ref, slab_ref, put)
    for copy in sends + placed:
        copy.wait()


def late_kernel(row_ref, tile_ref, picked_in, out_ref, picked_ref, *refs):
    buffer_ref, half_ref, slab_ref, sems = refs
    picked_copy = pltpu.make_async_copy(
        picked_in.at[pl.ds(0, picked_ref.shape[0])], picked_ref, sems.at[2 * buffer_ref.shape[0]]
    )
    picked_copy.start()
    copies = fetch(tile_ref, 0, buffer_ref, sems)
    picked_copy.wait()

    def put(item, at, rows):
        out_ref[item, at : at + rows.shape[0], :] = rows

    half_tiles(row_ref, 0, picked_ref, copies, buffer_ref, half_ref, slab_ref, put)


def serve_kernel(asked_ref, metric_in, out_ref, metric_ref, sem):
    copy = pltpu.make_async_copy(metric_in.at[pl.ds(0, metric_ref.shape[0])], metric_ref, sem)
    copy.start()
    copy.wait()
    lane = lax.broadcasted_iota(jnp.int32, out_ref.shape[1:], 1)
    for peer in range(out_ref.shape[0]):
        out_ref[peer] = jnp.where(
            lane < HALF, metric_ref[asked_ref[peer, 0]], metric_ref[asked_ref[peer, 1]]
        )


def term_kernel(first, first_slot, owner_ref, halves_ref, metric_ref, *refs):
    *before, out_ref, total = refs
    item_count, rows, _ = halves_ref.shape
    width = total.shape[0] // SLOTS
    depth = metric_ref.shape[1]
    steps = (item_count + 1) // 2
    groups = rows // width
    lane = lax.broadcasted_iota(jnp.int32, (depth, LANES), 1)
    rest = jnp.zeros((HALF - depth, LANES), jnp.float32)

    def placed(item):
        mine = owner_ref[item]
        slot = jnp.int32(0)
        for other in range(item):
            slot = slot | jnp.where(owner_ref[other] == mine, 1, 0)
        block = metric_ref[mine].astype(jnp.float32)
        turned = pltpu.roll(block, HALF, 1)
        low = jnp.where(slot == 0, block, turned)
        high = jnp.where(slot == 0, turned, block)
        stacked = [jnp.where(lane < HALF, low, 0.0), rest, jnp.where(lane < HALF, 0.0, high), rest]
        return jnp.concatenate(stacked, axis=0).astype(jnp.bfloat16)

    def spread(array):
        return jnp.concatenate(
            [array[g * width : (g + 1) * width, :] for g in range(groups)], axis=1
        )

    def term(item):
        if item >= item_count:
            return jnp.zeros((width, HALF), jnp.float32)
        halves = halves_ref[item]
        fitted = jnp.dot(halves, placed(first + item), preferred_element_type=jnp.float32)
        return lax.dot_general(
            spread(halves),
            spread(fitted.astype(jnp.bfloat16)),
            (((1,), (1,)), ((), ())),
            preferred_element_type=jnp.float32,
        )

    total[...] = before[0][...] if before else jnp.zeros_like(total)
    for step in range(steps):
        total[pl.ds(first_slot + step, width, stride=SLOTS), :] = jnp.concatenate(
            [term(step), term(step + steps)], axis=1
        )
    out_ref[...] = total[...].astype(out_ref.dtype)


def combine_kernel(parts_ref, pick_ref, out_ref):
    sources = parts_ref.shape[0]
    rows = parts_ref.shape[1] // SLOTS
    pairs = pick_ref.shape[0] // 8
    low = lax.broadcasted_iota(jnp.int32, (pairs, LANES), 1) < HALF
    for step in range(rows // 2):
        block = parts_ref[:, step * 2 * SLOTS : (step + 1) * 2 * SLOTS, :]
        summed = jnp.dot(
            pick_ref[...],
            block.reshape(sources * 2 * SLOTS, LANES),
            preferred_element_type=jnp.float32,
        )
        for parity in range(2):
            at = parity * 4 * pairs
            even = summed[at : at + pairs] + pltpu.roll(summed[at + pairs : at + 2 * pairs], HALF, 1)
            odd = summed[at + 3 * pairs : at + 4 * pairs] + pltpu.roll(
                summed[at + 2 * pairs : at + 3 * pairs], HALF, 1
            )
            out_ref[pl.ds(step * 2 + parity, pairs, stride=rows), :] = jnp.where(low, even, odd)


def final_kernel(parts_ref, out_ref):
    rows = out_ref.shape[1]
    summed = jnp.sum(parts_ref[...], axis=0)
    for side in range(out_ref.shape[0]):
        out_ref[side] = summed[:, side * HALF : (side + 1) * HALF]


def shards(tiles, coeff, support, row_block, col_block, owner, local_block, metric):
    item_count, width, columns = tiles.shape
    aux_width = metric.shape[1]
    orbitals = support.shape[1]
    aux_count = lax.axis_size("aux")
    pair_count = lax.axis_size("pair")
    groups = orbitals // 2
    vmem = pl.BlockSpec(memory_space=pltpu.VMEM)
    smem = pl.BlockSpec(memory_space=pltpu.SMEM)
    anywhere = pl.BlockSpec(memory_space=pl.ANY)
    small = pltpu.CompilerParams(vmem_limit_bytes=8 * MIB)
    row = lambda array: array.reshape(1, item_count)

    request = pl.pallas_call(
        request_kernel,
        out_shape=jax.ShapeDtypeStruct((aux_count, LANES), jnp.int32),
        in_specs=[vmem] * 3,
        out_specs=vmem,
        name="request",
    )(row(owner), row(local_block), row(col_block))
    asked = lax.all_to_all(
        request.reshape(aux_count, 1, LANES), "aux", split_axis=0, concat_axis=0, tiled=True
    ).reshape(aux_count, LANES)

    late_rows = groups * width
    by_aux = metric.transpose(1, 0, 2)
    depth = -(-aux_width // 8) * 8
    early_count = item_count * 3 // 11
    late_count = item_count - early_count

    def half_scratch(count):
        return [
            pltpu.VMEM((count, width, columns), jnp.bfloat16),
            pltpu.VMEM((2, orbitals, columns), jnp.float32),
            pltpu.VMEM((2, late_rows, LANES), jnp.float32),
            pltpu.SemaphoreType.DMA((2 * count + 2,)),
        ]

    def cost(count):
        return pl.CostEstimate(
            flops=2 * count * orbitals * width * columns,
            bytes_accessed=2 * count * (width * columns + late_rows * LANES),
            transcendentals=0,
        )

    padded_shape = (metric.shape[0], depth, LANES)
    picked_shape = (support.shape[0], orbitals, width)
    early, padded, picked = pl.pallas_call(
        early_kernel,
        out_shape=[
            jax.ShapeDtypeStruct((early_count, late_rows, LANES), jnp.bfloat16),
            jax.ShapeDtypeStruct((ROOM,) + padded_shape[1:], jnp.bfloat16),
            jax.ShapeDtypeStruct((ROOM,) + picked_shape[1:], jnp.bfloat16),
        ],
        in_specs=[smem, anywhere, vmem, vmem, vmem],
        out_specs=[anywhere] * 3,
        scratch_shapes=[
            pltpu.VMEM(padded_shape, jnp.bfloat16),
            pltpu.VMEM(picked_shape, jnp.bfloat16),
            pltpu.VMEM((aux_width * metric.shape[0], LANES), jnp.float32),
            pltpu.VMEM((early_count, late_rows, LANES), jnp.bfloat16),
        ]
        + half_scratch(early_count),
        compiler_params=pltpu.CompilerParams(vmem_limit_bytes=EARLY_LIMIT),
        cost_estimate=cost(early_count),
        name="early",
    )(row_block, tiles, by_aux, coeff, support)

    served = pl.pallas_call(
        serve_kernel,
        out_shape=jax.ShapeDtypeStruct((aux_count, depth, LANES), jnp.bfloat16),
        in_specs=[smem, anywhere],
        out_specs=vmem,
        scratch_shapes=[pltpu.VMEM(padded_shape, jnp.bfloat16), pltpu.SemaphoreType.DMA],
        compiler_params=pltpu.CompilerParams(vmem_limit_bytes=SERVE_LIMIT),
        name="serve",
    )(asked, padded)
    metric_tiles = lax.all_to_all(served, "aux", split_axis=0, concat_axis=0, tiled=True)

    picked, _ = lax.optimization_barrier((picked, served))
    late = pl.pallas_call(
        late_kernel,
        out_shape=jax.ShapeDtypeStruct((late_count, late_rows, LANES), jnp.bfloat16),
        in_specs=[smem, anywhere, anywhere],
        out_specs=vmem,
        scratch_shapes=[pltpu.VMEM(picked_shape, jnp.bfloat16)] + half_scratch(late_count),
        compiler_params=pltpu.CompilerParams(vmem_limit_bytes=LATE_LIMIT),
        cost_estimate=cost(late_count),
        name="late",
    )(row_block, tiles, picked)

    cols = asked[:, 32 : 32 + item_count]
    late_steps, early_steps = (late_count + 1) // 2, (early_count + 1) // 2

    def columns_of(*parts):
        taken = []
        for start, stop, size in parts:
            fill = ((0, 0), (0, size - (stop - start)))
            taken.append(jnp.pad(cols[:, start:stop], fill, constant_values=-1))
        return jnp.concatenate(taken, axis=1)

    spare = SLOTS - late_steps
    cols_a = columns_of(
        (0, late_steps, late_steps), (late_count, late_count + early_steps, spare)
    )
    cols_b = columns_of(
        (late_steps, late_count, late_steps), (late_count + early_steps, item_count, spare)
    )
    spread = lambda array: jnp.broadcast_to(array[:, None, :], (aux_count, 2, SLOTS)).reshape(1, -1)
    place = jnp.arange(8 * pair_count, dtype=jnp.int32)[:, None]
    block = 2 * (place % pair_count) + place // (2 * pair_count) % 2
    side_b = place // pair_count % 2 == 1
    parity = jnp.arange(aux_count * 2 * SLOTS, dtype=jnp.int32)[None, :] // SLOTS % 2
    hit = jnp.where(side_b, spread(cols_b) == block, spread(cols_a) == block)
    pick = jnp.where(hit & (parity == place // (4 * pair_count)), -1.0, 0.0).astype(jnp.bfloat16)

    def terms(first, first_slot, halves, before, dtype, name):
        return pl.pallas_call(
            functools.partial(term_kernel, first, first_slot),
            out_shape=jax.ShapeDtypeStruct((width * SLOTS, LANES), dtype),
            in_specs=[smem] + [vmem] * (2 + len(before)),
            out_specs=vmem,
            scratch_shapes=[pltpu.VMEM((width * SLOTS, LANES), jnp.float32)],
            compiler_params=pltpu.CompilerParams(vmem_limit_bytes=TERM_LIMIT),
            cost_estimate=pl.CostEstimate(
                flops=12 * halves.shape[0] * late_rows * LANES * (LANES + width),
                bytes_accessed=2 * halves.size,
                transcendentals=0,
            ),
            name=name,
        )(owner.reshape(item_count), halves, metric_tiles, *before)

    blocks = terms(0, 0, late, (), jnp.float32, "late_term")
    blocks = terms(late_count, late_steps, early, (blocks,), jnp.bfloat16, "early_term")
    rows = width // aux_count
    blocks, pick = lax.optimization_barrier((blocks, pick))
    parts = lax.all_to_all(
        blocks.reshape(aux_count, rows * SLOTS, LANES), "aux", split_axis=0, concat_axis=0, tiled=True
    )

    sums = pl.pallas_call(
        combine_kernel,
        out_shape=jax.ShapeDtypeStruct((pair_count * rows, LANES), jnp.float32),
        in_specs=[vmem] * 2,
        out_specs=vmem,
        compiler_params=small,
        name="combine",
    )(parts, pick)
    arrived = lax.all_to_all(
        sums.reshape(pair_count, rows, LANES), "pair", split_axis=0, concat_axis=0, tiled=True
    )
    return pl.pallas_call(
        final_kernel,
        out_shape=jax.ShapeDtypeStruct((2, rows, width), jnp.float32),
        in_specs=[vmem],
        out_specs=vmem,
        compiler_params=small,
        name="final",
    )(arrived)


def solution(mesh):
    return jax.shard_map(
        shards,
        mesh=mesh,
        in_specs=(
            P(("pair", "aux"), None, None),
            P("pair", None),
            P("pair", None),
            P(("pair", "aux")),
            P(("pair", "aux")),
            P(("pair", "aux"), None),
            P(("pair", "aux")),
            P("aux", None, None),
        ),
        out_specs=P("pair", "aux", None),
        check_vma=False,
    )
```

```python
import functools
import jax
import jax.numpy as jnp
from jax import lax
from jax.experimental import pallas as pl
from jax.experimental.pallas import tpu as pltpu
from jax.sharding import PartitionSpec as P

LANES = 128
HALF = 64
MIB = 1 << 20
ROOM = 700
EARLY_LIMIT = 61_000_000
STAGE_LIMIT = 51_000_000
LATE_LIMIT = 51_000_000
TERM_LIMIT = 51_000_000
SLOTS = 8


def request_kernel(owner_ref, local_ref, col_ref, out_ref):
    aux_count = out_ref.shape[0]
    shape = (aux_count, owner_ref.shape[1])
    position = lax.broadcasted_iota(jnp.int32, shape, 1)
    match = owner_ref[...] == lax.broadcasted_iota(jnp.int32, shape, 0)
    local = jnp.broadcast_to(local_ref[...], shape)
    first = jnp.min(jnp.where(match, position, LANES), axis=1, keepdims=True)
    last = jnp.max(jnp.where(match, position, -1), axis=1, keepdims=True)
    out_ref[...] = jnp.zeros_like(out_ref)
    out_ref[:, 0:1] = jnp.sum(jnp.where(position == first, local, 0), axis=1, keepdims=True)
    out_ref[:, 1:2] = jnp.sum(jnp.where(position == last, local, 0), axis=1, keepdims=True)
    out_ref[:, 32 : 32 + shape[1]] = jnp.broadcast_to(col_ref[...], shape)


def place(metric_ref, coeff_ref, support_ref, padded_ref, picked_ref, rows_ref):
    aux_width, blocks, _ = metric_ref.shape
    width = coeff_ref.shape[0] // support_ref.shape[0]
    shape = (coeff_ref.shape[1], support_ref.shape[1])
    for block in range(support_ref.shape[0]):
        onehot = support_ref[block : block + 1, :] == lax.broadcasted_iota(jnp.int32, shape, 0)
        chosen = jnp.dot(
            coeff_ref[block * width : (block + 1) * width, :],
            onehot.astype(jnp.float32).astype(jnp.bfloat16),
            preferred_element_type=jnp.float32,
        )
        picked_ref[block] = chosen.T.astype(jnp.bfloat16)
    rows_ref[...] = jnp.zeros_like(rows_ref)
    for p in range(aux_width):
        rows_ref[p * blocks : (p + 1) * blocks, :aux_width] = metric_ref[p].astype(jnp.float32)
    padded_ref[...] = jnp.zeros_like(padded_ref)
    for block in range(blocks):
        entry = rows_ref[pl.ds(block, aux_width, stride=blocks), :]
        padded_ref[block, :aux_width, :] = (entry + pltpu.roll(entry, HALF, 1)).astype(jnp.bfloat16)


def fetch(tile_ref, first, buffer_ref, sems):
    copies = [
        pltpu.make_async_copy(tile_ref.at[first + item], buffer_ref.at[item], sems.at[item])
        for item in range(buffer_ref.shape[0])
    ]
    for copy in copies:
        copy.start()
    return copies


def half_tiles(row_ref, first, picked_ref, copies, buffer_ref, half_ref, slab_ref, put):
    item_count, width, columns = buffer_ref.shape
    orbitals = picked_ref.shape[1]
    groups = orbitals // 2
    aux_width = columns // width
    lane = lax.broadcasted_iota(jnp.int32, (orbitals, LANES), 1)
    low = lane[:groups] < HALF

    def multiply(item):
        copies[item].wait()
        half_ref[item % 2] = jnp.dot(
            picked_ref[row_ref[first + item]], buffer_ref[item], preferred_element_type=jnp.float32
        )

    multiply(0)
    for item in range(item_count):
        if item + 1 < item_count:
            multiply(item + 1)
        half, slabs = half_ref.at[item % 2], slab_ref.at[item % 2]
        for nu in range(width):
            start = nu * aux_width
            base, shift = start // LANES * LANES, start % LANES
            window = half[:, base : base + LANES]
            if shift + aux_width > LANES:
                window = jnp.where(lane >= shift, window, half[:, base + LANES : base + 2 * LANES])
            front, back = window[:groups], window[groups:]
            if shift:
                front = pltpu.roll(front, LANES - shift, 1)
            if shift != HALF:
                back = pltpu.roll(back, (LANES + HALF - shift) % LANES, 1)
            slabs[nu * groups : (nu + 1) * groups, :] = jnp.where(low, front, back)
        for g in range(groups):
            put(item, g * width, slabs[pl.ds(g, width, stride=groups), :].astype(jnp.bfloat16))


def early_kernel(row_ref, tile_ref, metric_ref, coeff_ref, support_ref, *refs):
    out_ref, padded_out, picked_out, padded_ref, picked_ref, rows_ref, made_ref, *refs = refs
    buffer_ref, half_ref, slab_ref, sems = refs
    count = buffer_ref.shape[0]
    first = tile_ref.shape[0] - count
    copies = fetch(tile_ref, first, buffer_ref, sems)
    place(metric_ref, coeff_ref, support_ref, padded_ref, picked_ref, rows_ref)
    placed = [
        pltpu.make_async_copy(ref, out.at[pl.ds(0, ref.shape[0])], sems.at[2 * count + at])
        for at, (ref, out) in enumerate(((padded_ref, padded_out), (picked_ref, picked_out)))
    ]
    for copy in placed:
        copy.start()
    sends = [
        pltpu.make_async_copy(made_ref.at[item], out_ref.at[item], sems.at[count + item])
        for item in range(count)
    ]

    def put(item, at, rows):
        made_ref[item, at : at + rows.shape[0], :] = rows
        if at + rows.shape[0] == made_ref.shape[1]:
            sends[item].start()

    half_tiles(row_ref, first, picked_ref, copies, buffer_ref, half_ref, slab_ref, put)
    for copy in sends + placed:
        copy.wait()


def late_kernel(row_ref, tile_ref, picked_in, out_ref, picked_ref, *refs):
    buffer_ref, half_ref, slab_ref, sems = refs
    picked_copy = pltpu.make_async_copy(
        picked_in.at[pl.ds(0, picked_ref.shape[0])], picked_ref, sems.at[2 * buffer_ref.shape[0]]
    )
    picked_copy.start()
    copies = fetch(tile_ref, 0, buffer_ref, sems)
    picked_copy.wait()

    def put(item, at, rows):
        out_ref[item, at : at + rows.shape[0], :] = rows

    half_tiles(row_ref, 0, picked_ref, copies, buffer_ref, half_ref, slab_ref, put)


def stage_kernel(metric_in, metric_ref, sem):
    copy = pltpu.make_async_copy(metric_in.at[pl.ds(0, metric_ref.shape[0])], metric_ref, sem)
    copy.start()
    copy.wait()


def serve_kernel(asked_ref, metric_ref, out_ref):
    lane = lax.broadcasted_iota(jnp.int32, out_ref.shape[1:], 1)
    for peer in range(out_ref.shape[0]):
        out_ref[peer] = jnp.where(
            lane < HALF, metric_ref[asked_ref[peer, 0]], metric_ref[asked_ref[peer, 1]]
        )


def term_kernel(first, first_slot, owner_ref, halves_ref, metric_ref, *refs):
    *before, out_ref, total = refs
    item_count, rows, _ = halves_ref.shape
    width = total.shape[0] // SLOTS
    depth = metric_ref.shape[1]
    steps = (item_count + 1) // 2
    groups = rows // width
    lane = lax.broadcasted_iota(jnp.int32, (depth, LANES), 1)
    rest = jnp.zeros((HALF - depth, LANES), jnp.float32)

    def placed(item):
        mine = owner_ref[item]
        slot = jnp.int32(0)
        for other in range(item):
            slot = slot | jnp.where(owner_ref[other] == mine, 1, 0)
        block = metric_ref[mine].astype(jnp.float32)
        turned = pltpu.roll(block, HALF, 1)
        low = jnp.where(slot == 0, block, turned)
        high = jnp.where(slot == 0, turned, block)
        stacked = [jnp.where(lane < HALF, low, 0.0), rest, jnp.where(lane < HALF, 0.0, high), rest]
        return jnp.concatenate(stacked, axis=0).astype(jnp.bfloat16)

    def spread(array):
        return jnp.concatenate(
            [array[g * width : (g + 1) * width, :] for g in range(groups)], axis=1
        )

    def term(item):
        if item >= item_count:
            return jnp.zeros((width, HALF), jnp.float32)
        halves = halves_ref[item]
        fitted = jnp.dot(halves, placed(first + item), preferred_element_type=jnp.float32)
        return lax.dot_general(
            spread(halves),
            spread(fitted.astype(jnp.bfloat16)),
            (((1,), (1,)), ((), ())),
            preferred_element_type=jnp.float32,
        )

    total[...] = before[0][...] if before else jnp.zeros_like(total)
    for step in range(steps):
        total[pl.ds(first_slot + step, width, stride=SLOTS), :] = jnp.concatenate(
            [term(step), term(step + steps)], axis=1
        )
    out_ref[...] = total[...].astype(out_ref.dtype)


def combine_kernel(parts_ref, pick_ref, out_ref):
    sources = parts_ref.shape[0]
    rows = parts_ref.shape[1] // SLOTS
    pairs = pick_ref.shape[0] // 8
    low = lax.broadcasted_iota(jnp.int32, (pairs, LANES), 1) < HALF
    for step in range(rows // 2):
        block = parts_ref[:, step * 2 * SLOTS : (step + 1) * 2 * SLOTS, :]
        summed = jnp.dot(
            pick_ref[...],
            block.reshape(sources * 2 * SLOTS, LANES),
            preferred_element_type=jnp.float32,
        )
        for parity in range(2):
            at = parity * 4 * pairs
            even = summed[at : at + pairs] + pltpu.roll(summed[at + pairs : at + 2 * pairs], HALF, 1)
            odd = summed[at + 3 * pairs : at + 4 * pairs] + pltpu.roll(
                summed[at + 2 * pairs : at + 3 * pairs], HALF, 1
            )
            out_ref[pl.ds(step * 2 + parity, pairs, stride=rows), :] = jnp.where(low, even, odd)


def final_kernel(parts_ref, out_ref):
    rows = out_ref.shape[1]
    summed = jnp.sum(parts_ref[...], axis=0)
    for side in range(out_ref.shape[0]):
        out_ref[side] = summed[:, side * HALF : (side + 1) * HALF]


def shards(tiles, coeff, support, row_block, col_block, owner, local_block, metric):
    item_count, width, columns = tiles.shape
    aux_width = metric.shape[1]
    orbitals = support.shape[1]
    aux_count = lax.axis_size("aux")
    pair_count = lax.axis_size("pair")
    groups = orbitals // 2
    vmem = pl.BlockSpec(memory_space=pltpu.VMEM)
    smem = pl.BlockSpec(memory_space=pltpu.SMEM)
    anywhere = pl.BlockSpec(memory_space=pl.ANY)
    small = pltpu.CompilerParams(vmem_limit_bytes=8 * MIB)
    row = lambda array: array.reshape(1, item_count)

    request = pl.pallas_call(
        request_kernel,
        out_shape=jax.ShapeDtypeStruct((aux_count, LANES), jnp.int32),
        in_specs=[vmem] * 3,
        out_specs=vmem,
        name="request",
    )(row(owner), row(local_block), row(col_block))
    asked = lax.all_to_all(
        request.reshape(aux_count, 1, LANES), "aux", split_axis=0, concat_axis=0, tiled=True
    ).reshape(aux_count, LANES)

    late_rows = groups * width
    by_aux = metric.transpose(1, 0, 2)
    depth = -(-aux_width // 8) * 8
    early_count = item_count * 3 // 11
    late_count = item_count - early_count

    def half_scratch(count):
        return [
            pltpu.VMEM((count, width, columns), jnp.bfloat16),
            pltpu.VMEM((2, orbitals, columns), jnp.float32),
            pltpu.VMEM((2, late_rows, LANES), jnp.float32),
            pltpu.SemaphoreType.DMA((2 * count + 2,)),
        ]

    def cost(count):
        return pl.CostEstimate(
            flops=2 * count * orbitals * width * columns,
            bytes_accessed=2 * count * (width * columns + late_rows * LANES),
            transcendentals=0,
        )

    padded_shape = (metric.shape[0], depth, LANES)
    picked_shape = (support.shape[0], orbitals, width)
    early, padded, picked = pl.pallas_call(
        early_kernel,
        out_shape=[
            jax.ShapeDtypeStruct((early_count, late_rows, LANES), jnp.bfloat16),
            jax.ShapeDtypeStruct((ROOM,) + padded_shape[1:], jnp.bfloat16),
            jax.ShapeDtypeStruct((ROOM,) + picked_shape[1:], jnp.bfloat16),
        ],
        in_specs=[smem, anywhere, vmem, vmem, vmem],
        out_specs=[anywhere] * 3,
        scratch_shapes=[
            pltpu.VMEM(padded_shape, jnp.bfloat16),
            pltpu.VMEM(picked_shape, jnp.bfloat16),
            pltpu.VMEM((aux_width * metric.shape[0], LANES), jnp.float32),
            pltpu.VMEM((early_count, late_rows, LANES), jnp.bfloat16),
        ]
        + half_scratch(early_count),
        compiler_params=pltpu.CompilerParams(vmem_limit_bytes=EARLY_LIMIT),
        cost_estimate=cost(early_count),
        name="early",
    )(row_block, tiles, by_aux, coeff, support)

    padded = pl.pallas_call(
        stage_kernel,
        out_shape=jax.ShapeDtypeStruct(padded_shape, jnp.bfloat16),
        in_specs=[anywhere],
        out_specs=vmem,
        scratch_shapes=[pltpu.SemaphoreType.DMA],
        compiler_params=pltpu.CompilerParams(vmem_limit_bytes=STAGE_LIMIT),
        name="stage",
    )(padded)

    served = pl.pallas_call(
        serve_kernel,
        out_shape=jax.ShapeDtypeStruct((aux_count, depth, LANES), jnp.bfloat16),
        in_specs=[smem, vmem],
        out_specs=vmem,
        compiler_params=pltpu.CompilerParams(vmem_limit_bytes=8 * MIB),
        name="serve",
    )(asked, padded)
    metric_tiles = lax.all_to_all(served, "aux", split_axis=0, concat_axis=0, tiled=True)

    picked, _ = lax.optimization_barrier((picked, served))
    late = pl.pallas_call(
        late_kernel,
        out_shape=jax.ShapeDtypeStruct((late_count, late_rows, LANES), jnp.bfloat16),
        in_specs=[smem, anywhere, anywhere],
        out_specs=vmem,
        scratch_shapes=[pltpu.VMEM(picked_shape, jnp.bfloat16)] + half_scratch(late_count),
        compiler_params=pltpu.CompilerParams(vmem_limit_bytes=LATE_LIMIT),
        cost_estimate=cost(late_count),
        name="late",
    )(row_block, tiles, picked)

    cols = asked[:, 32 : 32 + item_count]
    late_steps, early_steps = (late_count + 1) // 2, (early_count + 1) // 2

    def columns_of(*parts):
        taken = []
        for start, stop, size in parts:
            fill = ((0, 0), (0, size - (stop - start)))
            taken.append(jnp.pad(cols[:, start:stop], fill, constant_values=-1))
        return jnp.concatenate(taken, axis=1)

    spare = SLOTS - late_steps
    cols_a = columns_of(
        (0, late_steps, late_steps), (late_count, late_count + early_steps, spare)
    )
    cols_b = columns_of(
        (late_steps, late_count, late_steps), (late_count + early_steps, item_count, spare)
    )
    spread = lambda array: jnp.broadcast_to(array[:, None, :], (aux_count, 2, SLOTS)).reshape(1, -1)
    place = jnp.arange(8 * pair_count, dtype=jnp.int32)[:, None]
    block = 2 * (place % pair_count) + place // (2 * pair_count) % 2
    side_b = place // pair_count % 2 == 1
    parity = jnp.arange(aux_count * 2 * SLOTS, dtype=jnp.int32)[None, :] // SLOTS % 2
    hit = jnp.where(side_b, spread(cols_b) == block, spread(cols_a) == block)
    pick = jnp.where(hit & (parity == place // (4 * pair_count)), -1.0, 0.0).astype(jnp.bfloat16)

    def terms(first, first_slot, halves, before, dtype, name):
        return pl.pallas_call(
            functools.partial(term_kernel, first, first_slot),
            out_shape=jax.ShapeDtypeStruct((width * SLOTS, LANES), dtype),
            in_specs=[smem] + [vmem] * (2 + len(before)),
            out_specs=vmem,
            scratch_shapes=[pltpu.VMEM((width * SLOTS, LANES), jnp.float32)],
            compiler_params=pltpu.CompilerParams(vmem_limit_bytes=TERM_LIMIT),
            cost_estimate=pl.CostEstimate(
                flops=12 * halves.shape[0] * late_rows * LANES * (LANES + width),
                bytes_accessed=2 * halves.size,
                transcendentals=0,
            ),
            name=name,
        )(owner.reshape(item_count), halves, metric_tiles, *before)

    blocks = terms(0, 0, late, (), jnp.float32, "late_term")
    blocks = terms(late_count, late_steps, early, (blocks,), jnp.bfloat16, "early_term")
    rows = width // aux_count
    blocks, pick = lax.optimization_barrier((blocks, pick))
    parts = lax.all_to_all(
        blocks.reshape(aux_count, rows * SLOTS, LANES), "aux", split_axis=0, concat_axis=0, tiled=True
    )

    sums = pl.pallas_call(
        combine_kernel,
        out_shape=jax.ShapeDtypeStruct((pair_count * rows, LANES), jnp.float32),
        in_specs=[vmem] * 2,
        out_specs=vmem,
        compiler_params=small,
        name="combine",
    )(parts, pick)
    arrived = lax.all_to_all(
        sums.reshape(pair_count, rows, LANES), "pair", split_axis=0, concat_axis=0, tiled=True
    )
    return pl.pallas_call(
        final_kernel,
        out_shape=jax.ShapeDtypeStruct((2, rows, width), jnp.float32),
        in_specs=[vmem],
        out_specs=vmem,
        compiler_params=small,
        name="final",
    )(arrived)


def solution(mesh):
    return jax.shard_map(
        shards,
        mesh=mesh,
        in_specs=(
            P(("pair", "aux"), None, None),
            P("pair", None),
            P("pair", None),
            P(("pair", "aux")),
            P(("pair", "aux")),
            P(("pair", "aux"), None),
            P(("pair", "aux")),
            P("aux", None, None),
        ),
        out_specs=P("pair", "aux", None),
        check_vma=False,
    )
```

```python
import functools
import jax
import jax.numpy as jnp
from jax import lax
from jax.experimental import pallas as pl
from jax.experimental.pallas import tpu as pltpu
from jax.sharding import PartitionSpec as P

LANES = 128
HALF = 64
MIB = 1 << 20
ROOM = 700
EARLY_LIMIT = 61_000_000
STAGE_LIMIT = 51_000_000
LATE_LIMIT = 51_000_000
TERM_LIMIT = 51_000_000
SLOTS = 8


def request_kernel(owner_ref, local_ref, col_ref, out_ref):
    aux_count = out_ref.shape[0]
    shape = (aux_count, owner_ref.shape[1])
    position = lax.broadcasted_iota(jnp.int32, shape, 1)
    match = owner_ref[...] == lax.broadcasted_iota(jnp.int32, shape, 0)
    local = jnp.broadcast_to(local_ref[...], shape)
    first = jnp.min(jnp.where(match, position, LANES), axis=1, keepdims=True)
    last = jnp.max(jnp.where(match, position, -1), axis=1, keepdims=True)
    out_ref[...] = jnp.zeros_like(out_ref)
    out_ref[:, 0:1] = jnp.sum(jnp.where(position == first, local, 0), axis=1, keepdims=True)
    out_ref[:, 1:2] = jnp.sum(jnp.where(position == last, local, 0), axis=1, keepdims=True)
    out_ref[:, 32 : 32 + shape[1]] = jnp.broadcast_to(col_ref[...], shape)


def place(metric_ref, coeff_ref, support_ref, padded_ref, picked_ref, rows_ref):
    aux_width, blocks, _ = metric_ref.shape
    width = coeff_ref.shape[0] // support_ref.shape[0]
    shape = (coeff_ref.shape[1], support_ref.shape[1])
    for block in range(support_ref.shape[0]):
        onehot = support_ref[block : block + 1, :] == lax.broadcasted_iota(jnp.int32, shape, 0)
        chosen = jnp.dot(
            coeff_ref[block * width : (block + 1) * width, :],
            onehot.astype(jnp.float32).astype(jnp.bfloat16),
            preferred_element_type=jnp.float32,
        )
        picked_ref[block] = chosen.T.astype(jnp.bfloat16)
    rows_ref[...] = jnp.zeros_like(rows_ref)
    for p in range(aux_width):
        rows_ref[p * blocks : (p + 1) * blocks, :aux_width] = metric_ref[p].astype(jnp.float32)
    padded_ref[...] = jnp.zeros_like(padded_ref)
    for block in range(blocks):
        entry = rows_ref[pl.ds(block, aux_width, stride=blocks), :]
        padded_ref[block, :aux_width, :] = (entry + pltpu.roll(entry, HALF, 1)).astype(jnp.bfloat16)


def fetch(tile_ref, first, buffer_ref, sems):
    copies = [
        pltpu.make_async_copy(tile_ref.at[first + item], buffer_ref.at[item], sems.at[item])
        for item in range(buffer_ref.shape[0])
    ]
    for copy in copies:
        copy.start()
    return copies


def half_tiles(row_ref, first, picked_ref, copies, buffer_ref, half_ref, slab_ref, put):
    item_count, width, columns = buffer_ref.shape
    orbitals = picked_ref.shape[1]
    groups = orbitals // 2
    aux_width = columns // width
    lane = lax.broadcasted_iota(jnp.int32, (orbitals, LANES), 1)
    low = lane[:groups] < HALF

    def multiply(item):
        copies[item].wait()
        half_ref[item % 2] = jnp.dot(
            picked_ref[row_ref[first + item]], buffer_ref[item], preferred_element_type=jnp.float32
        )

    multiply(0)
    for item in range(item_count):
        if item + 1 < item_count:
            multiply(item + 1)
        half, slabs = half_ref.at[item % 2], slab_ref.at[item % 2]
        for nu in range(width):
            start = nu * aux_width
            base, shift = start // LANES * LANES, start % LANES
            window = half[:, base : base + LANES]
            if shift + aux_width > LANES:
                window = jnp.where(lane >= shift, window, half[:, base + LANES : base + 2 * LANES])
            front, back = window[:groups], window[groups:]
            if shift:
                front = pltpu.roll(front, LANES - shift, 1)
            if shift != HALF:
                back = pltpu.roll(back, (LANES + HALF - shift) % LANES, 1)
            slabs[nu * groups : (nu + 1) * groups, :] = jnp.where(low, front, back)
        for g in range(groups):
            put(item, g * width, slabs[pl.ds(g, width, stride=groups), :].astype(jnp.bfloat16))


def early_kernel(row_ref, tile_ref, metric_ref, coeff_ref, support_ref, *refs):
    out_ref, padded_out, picked_out, padded_ref, picked_ref, rows_ref, made_ref, *refs = refs
    buffer_ref, half_ref, slab_ref, sems = refs
    count = buffer_ref.shape[0]
    first = tile_ref.shape[0] - count
    copies = fetch(tile_ref, first, buffer_ref, sems)
    place(metric_ref, coeff_ref, support_ref, padded_ref, picked_ref, rows_ref)
    placed = [
        pltpu.make_async_copy(ref, out.at[pl.ds(0, ref.shape[0])], sems.at[2 * count + at])
        for at, (ref, out) in enumerate(((padded_ref, padded_out), (picked_ref, picked_out)))
    ]
    for copy in placed:
        copy.start()
    sends = [
        pltpu.make_async_copy(made_ref.at[item], out_ref.at[item], sems.at[count + item])
        for item in range(count)
    ]

    def put(item, at, rows):
        made_ref[item, at : at + rows.shape[0], :] = rows
        if at + rows.shape[0] == made_ref.shape[1]:
            sends[item].start()

    half_tiles(row_ref, first, picked_ref, copies, buffer_ref, half_ref, slab_ref, put)
    for copy in sends + placed:
        copy.wait()


def late_kernel(row_ref, tile_ref, picked_in, out_ref, picked_ref, *refs):
    buffer_ref, half_ref, slab_ref, sems = refs
    picked_copy = pltpu.make_async_copy(
        picked_in.at[pl.ds(0, picked_ref.shape[0])], picked_ref, sems.at[2 * buffer_ref.shape[0]]
    )
    picked_copy.start()
    copies = fetch(tile_ref, 0, buffer_ref, sems)
    picked_copy.wait()

    def put(item, at, rows):
        out_ref[item, at : at + rows.shape[0], :] = rows

    half_tiles(row_ref, 0, picked_ref, copies, buffer_ref, half_ref, slab_ref, put)


def stage_kernel(metric_in, metric_ref, sem):
    copy = pltpu.make_async_copy(metric_in.at[pl.ds(0, metric_ref.shape[0])], metric_ref, sem)
    copy.start()
    copy.wait()


def serve_kernel(asked_ref, metric_ref, out_ref):
    lane = lax.broadcasted_iota(jnp.int32, out_ref.shape[1:], 1)
    for peer in range(out_ref.shape[0]):
        out_ref[peer] = jnp.where(
            lane < HALF, metric_ref[asked_ref[peer, 0]], metric_ref[asked_ref[peer, 1]]
        )


def term_kernel(first, first_slot, owner_ref, halves_ref, metric_ref, *refs):
    *before, out_ref, total = refs
    item_count, rows, _ = halves_ref.shape
    width = total.shape[0] // SLOTS
    depth = metric_ref.shape[1]
    steps = (item_count + 1) // 2
    groups = rows // width
    lane = lax.broadcasted_iota(jnp.int32, (depth, LANES), 1)
    rest = jnp.zeros((HALF - depth, LANES), jnp.float32)

    def placed(item):
        mine = owner_ref[item]
        slot = jnp.int32(0)
        for other in range(item):
            slot = slot | jnp.where(owner_ref[other] == mine, 1, 0)
        block = metric_ref[mine].astype(jnp.float32)
        turned = pltpu.roll(block, HALF, 1)
        low = jnp.where(slot == 0, block, turned)
        high = jnp.where(slot == 0, turned, block)
        stacked = [jnp.where(lane < HALF, low, 0.0), rest, jnp.where(lane < HALF, 0.0, high), rest]
        return jnp.concatenate(stacked, axis=0).astype(jnp.bfloat16)

    def spread(array):
        return jnp.concatenate(
            [array[g * width : (g + 1) * width, :] for g in range(groups)], axis=1
        )

    def term(item):
        if item >= item_count:
            return jnp.zeros((width, HALF), jnp.float32)
        halves = halves_ref[item]
        fitted = jnp.dot(halves, placed(first + item), preferred_element_type=jnp.float32)
        return lax.dot_general(
            spread(halves),
            spread(fitted.astype(jnp.bfloat16)),
            (((1,), (1,)), ((), ())),
            preferred_element_type=jnp.float32,
        )

    total[...] = before[0][...] if before else jnp.zeros_like(total)
    for step in range(steps):
        total[pl.ds(first_slot + step, width, stride=SLOTS), :] = jnp.concatenate(
            [term(step), term(step + steps)], axis=1
        )
    out_ref[...] = total[...].astype(out_ref.dtype)


def combine_kernel(parts_ref, pick_ref, out_ref, sum_ref):
    sources = parts_ref.shape[0]
    rows = parts_ref.shape[1] // SLOTS
    pairs = pick_ref.shape[0] // 8
    low = lax.broadcasted_iota(jnp.int32, (pairs, LANES), 1) < HALF
    for step in range(rows // 2):
        block = parts_ref[:, step * 2 * SLOTS : (step + 1) * 2 * SLOTS, :]
        summed = jnp.dot(
            pick_ref[...],
            block.reshape(sources * 2 * SLOTS, LANES),
            preferred_element_type=jnp.float32,
        )
        for parity in range(2):
            at = parity * 4 * pairs
            even = summed[at : at + pairs] + pltpu.roll(summed[at + pairs : at + 2 * pairs], HALF, 1)
            odd = summed[at + 3 * pairs : at + 4 * pairs] + pltpu.roll(
                summed[at + 2 * pairs : at + 3 * pairs], HALF, 1
            )
            sum_ref[pl.ds(step * 2 + parity, pairs, stride=rows), :] = jnp.where(low, even, odd)
    out_ref[...] = sum_ref[...].astype(out_ref.dtype)


def final_kernel(parts_ref, out_ref):
    rows = out_ref.shape[1]
    parts = parts_ref[...].astype(jnp.float32)
    step = 8 // rows * rows
    summed = parts[:step]
    for at in range(step, parts.shape[0], step):
        summed = summed + parts[at : at + step]
    summed = sum(summed[at : at + rows] for at in range(0, step, rows))
    for side in range(out_ref.shape[0]):
        out_ref[side] = summed[:, side * HALF : (side + 1) * HALF]


def shards(tiles, coeff, support, row_block, col_block, owner, local_block, metric):
    item_count, width, columns = tiles.shape
    aux_width = metric.shape[1]
    orbitals = support.shape[1]
    aux_count = lax.axis_size("aux")
    pair_count = lax.axis_size("pair")
    groups = orbitals // 2
    vmem = pl.BlockSpec(memory_space=pltpu.VMEM)
    smem = pl.BlockSpec(memory_space=pltpu.SMEM)
    anywhere = pl.BlockSpec(memory_space=pl.ANY)
    small = pltpu.CompilerParams(vmem_limit_bytes=8 * MIB)
    row = lambda array: array.reshape(1, item_count)

    request = pl.pallas_call(
        request_kernel,
        out_shape=jax.ShapeDtypeStruct((aux_count, LANES), jnp.int32),
        in_specs=[vmem] * 3,
        out_specs=vmem,
        name="request",
    )(row(owner), row(local_block), row(col_block))
    asked = lax.all_to_all(
        request.reshape(aux_count, 1, LANES), "aux", split_axis=0, concat_axis=0, tiled=True
    ).reshape(aux_count, LANES)

    late_rows = groups * width
    by_aux = metric.transpose(1, 0, 2)
    depth = -(-aux_width // 8) * 8
    early_count = item_count * 3 // 11
    late_count = item_count - early_count

    def half_scratch(count):
        return [
            pltpu.VMEM((count, width, columns), jnp.bfloat16),
            pltpu.VMEM((2, orbitals, columns), jnp.float32),
            pltpu.VMEM((2, late_rows, LANES), jnp.float32),
            pltpu.SemaphoreType.DMA((2 * count + 2,)),
        ]

    def cost(count):
        return pl.CostEstimate(
            flops=2 * count * orbitals * width * columns,
            bytes_accessed=2 * count * (width * columns + late_rows * LANES),
            transcendentals=0,
        )

    padded_shape = (metric.shape[0], depth, LANES)
    picked_shape = (support.shape[0], orbitals, width)
    early, padded, picked = pl.pallas_call(
        early_kernel,
        out_shape=[
            jax.ShapeDtypeStruct((early_count, late_rows, LANES), jnp.bfloat16),
            jax.ShapeDtypeStruct((ROOM,) + padded_shape[1:], jnp.bfloat16),
            jax.ShapeDtypeStruct((ROOM,) + picked_shape[1:], jnp.bfloat16),
        ],
        in_specs=[smem, anywhere, vmem, vmem, vmem],
        out_specs=[anywhere] * 3,
        scratch_shapes=[
            pltpu.VMEM(padded_shape, jnp.bfloat16),
            pltpu.VMEM(picked_shape, jnp.bfloat16),
            pltpu.VMEM((aux_width * metric.shape[0], LANES), jnp.float32),
            pltpu.VMEM((early_count, late_rows, LANES), jnp.bfloat16),
        ]
        + half_scratch(early_count),
        compiler_params=pltpu.CompilerParams(vmem_limit_bytes=EARLY_LIMIT),
        cost_estimate=cost(early_count),
        name="early",
    )(row_block, tiles, by_aux, coeff, support)

    padded = pl.pallas_call(
        stage_kernel,
        out_shape=jax.ShapeDtypeStruct(padded_shape, jnp.bfloat16),
        in_specs=[anywhere],
        out_specs=vmem,
        scratch_shapes=[pltpu.SemaphoreType.DMA],
        compiler_params=pltpu.CompilerParams(vmem_limit_bytes=STAGE_LIMIT),
        name="stage",
    )(padded)

    served = pl.pallas_call(
        serve_kernel,
        out_shape=jax.ShapeDtypeStruct((aux_count, depth, LANES), jnp.bfloat16),
        in_specs=[smem, vmem],
        out_specs=vmem,
        compiler_params=pltpu.CompilerParams(vmem_limit_bytes=8 * MIB),
        name="serve",
    )(asked, padded)
    metric_tiles = lax.all_to_all(served, "aux", split_axis=0, concat_axis=0, tiled=True)

    picked, _ = lax.optimization_barrier((picked, served))
    late = pl.pallas_call(
        late_kernel,
        out_shape=jax.ShapeDtypeStruct((late_count, late_rows, LANES), jnp.bfloat16),
        in_specs=[smem, anywhere, anywhere],
        out_specs=vmem,
        scratch_shapes=[pltpu.VMEM(picked_shape, jnp.bfloat16)] + half_scratch(late_count),
        compiler_params=pltpu.CompilerParams(vmem_limit_bytes=LATE_LIMIT),
        cost_estimate=cost(late_count),
        name="late",
    )(row_block, tiles, picked)

    cols = asked[:, 32 : 32 + item_count]
    late_steps, early_steps = (late_count + 1) // 2, (early_count + 1) // 2

    def columns_of(*parts):
        taken = []
        for start, stop, size in parts:
            fill = ((0, 0), (0, size - (stop - start)))
            taken.append(jnp.pad(cols[:, start:stop], fill, constant_values=-1))
        return jnp.concatenate(taken, axis=1)

    spare = SLOTS - late_steps
    cols_a = columns_of(
        (0, late_steps, late_steps), (late_count, late_count + early_steps, spare)
    )
    cols_b = columns_of(
        (late_steps, late_count, late_steps), (late_count + early_steps, item_count, spare)
    )
    spread = lambda array: jnp.broadcast_to(array[:, None, :], (aux_count, 2, SLOTS)).reshape(1, -1)
    place = jnp.arange(8 * pair_count, dtype=jnp.int32)[:, None]
    block = 2 * (place % pair_count) + place // (2 * pair_count) % 2
    side_b = place // pair_count % 2 == 1
    parity = jnp.arange(aux_count * 2 * SLOTS, dtype=jnp.int32)[None, :] // SLOTS % 2
    hit = jnp.where(side_b, spread(cols_b) == block, spread(cols_a) == block)
    pick = jnp.where(hit & (parity == place // (4 * pair_count)), -1.0, 0.0).astype(jnp.bfloat16)

    def terms(first, first_slot, halves, before, dtype, name):
        return pl.pallas_call(
            functools.partial(term_kernel, first, first_slot),
            out_shape=jax.ShapeDtypeStruct((width * SLOTS, LANES), dtype),
            in_specs=[smem] + [vmem] * (2 + len(before)),
            out_specs=vmem,
            scratch_shapes=[pltpu.VMEM((width * SLOTS, LANES), jnp.float32)],
            compiler_params=pltpu.CompilerParams(vmem_limit_bytes=TERM_LIMIT),
            cost_estimate=pl.CostEstimate(
                flops=12 * halves.shape[0] * late_rows * LANES * (LANES + width),
                bytes_accessed=2 * halves.size,
                transcendentals=0,
            ),
            name=name,
        )(owner.reshape(item_count), halves, metric_tiles, *before)

    blocks = terms(0, 0, late, (), jnp.float32, "late_term")
    blocks = terms(late_count, late_steps, early, (blocks,), jnp.bfloat16, "early_term")
    rows = width // aux_count
    blocks, pick = lax.optimization_barrier((blocks, pick))
    parts = lax.all_to_all(
        blocks.reshape(aux_count, rows * SLOTS, LANES), "aux", split_axis=0, concat_axis=0, tiled=True
    )

    sums = pl.pallas_call(
        combine_kernel,
        out_shape=jax.ShapeDtypeStruct((pair_count * rows, LANES), jnp.bfloat16),
        in_specs=[vmem] * 2,
        out_specs=vmem,
        scratch_shapes=[pltpu.VMEM((pair_count * rows, LANES), jnp.float32)],
        compiler_params=small,
        name="combine",
    )(parts, pick)
    arrived = lax.all_to_all(
        sums.reshape(pair_count, rows, LANES), "pair", split_axis=0, concat_axis=0, tiled=True
    )
    return pl.pallas_call(
        final_kernel,
        out_shape=jax.ShapeDtypeStruct((2, rows, width), jnp.float32),
        in_specs=[vmem],
        out_specs=vmem,
        compiler_params=small,
        name="final",
    )(arrived.reshape(pair_count * rows, LANES))


def solution(mesh):
    return jax.shard_map(
        shards,
        mesh=mesh,
        in_specs=(
            P(("pair", "aux"), None, None),
            P("pair", None),
            P("pair", None),
            P(("pair", "aux")),
            P(("pair", "aux")),
            P(("pair", "aux"), None),
            P(("pair", "aux")),
            P("aux", None, None),
        ),
        out_specs=P("pair", "aux", None),
        check_vma=False,
    )
```

```python
import functools
import jax
import jax.numpy as jnp
from jax import lax
from jax.experimental import pallas as pl
from jax.experimental.pallas import tpu as pltpu
from jax.sharding import PartitionSpec as P

LANES = 128
HALF = 64
MIB = 1 << 20
ROOM = 700
EARLY_LIMIT = 61_000_000
TILES_LIMIT = 55_400_000
LATE_LIMIT = 51_000_000
TERM_LIMIT = 51_000_000
SLOTS = 8


def request_kernel(owner_ref, local_ref, col_ref, out_ref):
    aux_count = out_ref.shape[0]
    shape = (aux_count, owner_ref.shape[1])
    position = lax.broadcasted_iota(jnp.int32, shape, 1)
    match = owner_ref[...] == lax.broadcasted_iota(jnp.int32, shape, 0)
    local = jnp.broadcast_to(local_ref[...], shape)
    first = jnp.min(jnp.where(match, position, LANES), axis=1, keepdims=True)
    last = jnp.max(jnp.where(match, position, -1), axis=1, keepdims=True)
    out_ref[...] = jnp.zeros_like(out_ref)
    out_ref[:, 0:1] = jnp.sum(jnp.where(position == first, local, 0), axis=1, keepdims=True)
    out_ref[:, 1:2] = jnp.sum(jnp.where(position == last, local, 0), axis=1, keepdims=True)
    out_ref[:, 32 : 32 + shape[1]] = jnp.broadcast_to(col_ref[...], shape)


def place(metric_ref, coeff_ref, support_ref, padded_ref, picked_ref, rows_ref):
    aux_width, blocks, _ = metric_ref.shape
    width = coeff_ref.shape[0] // support_ref.shape[0]
    shape = (coeff_ref.shape[1], support_ref.shape[1])
    for block in range(support_ref.shape[0]):
        onehot = support_ref[block : block + 1, :] == lax.broadcasted_iota(jnp.int32, shape, 0)
        chosen = jnp.dot(
            coeff_ref[block * width : (block + 1) * width, :],
            onehot.astype(jnp.float32).astype(jnp.bfloat16),
            preferred_element_type=jnp.float32,
        )
        picked_ref[block] = chosen.T.astype(jnp.bfloat16)
    rows_ref[...] = jnp.zeros_like(rows_ref)
    for p in range(aux_width):
        rows_ref[p * blocks : (p + 1) * blocks, :aux_width] = metric_ref[p].astype(jnp.float32)
    padded_ref[...] = jnp.zeros_like(padded_ref)
    for block in range(blocks):
        entry = rows_ref[pl.ds(block, aux_width, stride=blocks), :]
        padded_ref[block, :aux_width, :] = (entry + pltpu.roll(entry, HALF, 1)).astype(jnp.bfloat16)


def fetch(tile_ref, first, buffer_ref, sems):
    copies = [
        pltpu.make_async_copy(tile_ref.at[first + item], buffer_ref.at[item], sems.at[item])
        for item in range(buffer_ref.shape[0])
    ]
    for copy in copies:
        copy.start()
    return copies


def half_tiles(picked_ref, copies, buffer_ref, half_ref, slab_ref, put):
    item_count, width, columns = buffer_ref.shape
    orbitals = picked_ref.shape[1]
    groups = orbitals // 2
    aux_width = columns // width
    lane = lax.broadcasted_iota(jnp.int32, (orbitals, LANES), 1)
    low = lane[:groups] < HALF

    def multiply(item):
        copies[item].wait()
        half_ref[item % 2] = jnp.dot(
            picked_ref[item], buffer_ref[item], preferred_element_type=jnp.float32
        )

    multiply(0)
    for item in range(item_count):
        if item + 1 < item_count:
            multiply(item + 1)
        half, slabs = half_ref.at[item % 2], slab_ref.at[item % 2]
        for nu in range(width):
            start = nu * aux_width
            base, shift = start // LANES * LANES, start % LANES
            window = half[:, base : base + LANES]
            if shift + aux_width > LANES:
                window = jnp.where(lane >= shift, window, half[:, base + LANES : base + 2 * LANES])
            front, back = window[:groups], window[groups:]
            if shift:
                front = pltpu.roll(front, LANES - shift, 1)
            if shift != HALF:
                back = pltpu.roll(back, (LANES + HALF - shift) % LANES, 1)
            slabs[nu * groups : (nu + 1) * groups, :] = jnp.where(low, front, back)
        for g in range(groups):
            put(item, g * width, slabs[pl.ds(g, width, stride=groups), :].astype(jnp.bfloat16))


def place_kernel(row_ref, metric_ref, coeff_ref, support_ref, padded_ref, picked_out, *refs):
    picked_ref, item_ref, rows_ref, sem = refs
    place(metric_ref, coeff_ref, support_ref, padded_ref, picked_ref, rows_ref)
    for item in range(item_ref.shape[0]):
        item_ref[item] = picked_ref[row_ref[item]]
    copy = pltpu.make_async_copy(item_ref, picked_out.at[pl.ds(0, item_ref.shape[0])], sem)
    copy.start()
    copy.wait()


def early_kernel(tile_ref, picked_in, out_ref, picked_ref, made_ref, *refs):
    buffer_ref, half_ref, slab_ref, sems = refs
    count = buffer_ref.shape[0]
    first = tile_ref.shape[0] - count
    picked_copy = pltpu.make_async_copy(
        picked_in.at[pl.ds(first, count)], picked_ref, sems.at[2 * count]
    )
    picked_copy.start()
    copies = fetch(tile_ref, first, buffer_ref, sems)
    picked_copy.wait()
    sends = [
        pltpu.make_async_copy(made_ref.at[item], out_ref.at[item], sems.at[count + item])
        for item in range(count)
    ]

    def put(item, at, rows):
        made_ref[item, at : at + rows.shape[0], :] = rows
        if at + rows.shape[0] == made_ref.shape[1]:
            sends[item].start()

    half_tiles(picked_ref, copies, buffer_ref, half_ref, slab_ref, put)
    for copy in sends:
        copy.wait()


def late_kernel(tile_ref, picked_in, out_ref, picked_ref, *refs):
    buffer_ref, half_ref, slab_ref, sems = refs
    picked_copy = pltpu.make_async_copy(
        picked_in.at[pl.ds(0, picked_ref.shape[0])], picked_ref, sems.at[2 * buffer_ref.shape[0]]
    )
    picked_copy.start()
    copies = fetch(tile_ref, 0, buffer_ref, sems)
    picked_copy.wait()

    def put(item, at, rows):
        out_ref[item, at : at + rows.shape[0], :] = rows

    half_tiles(picked_ref, copies, buffer_ref, half_ref, slab_ref, put)


def serve_kernel(asked_ref, metric_ref, out_ref):
    lane = lax.broadcasted_iota(jnp.int32, out_ref.shape[1:], 1)
    for peer in range(out_ref.shape[0]):
        out_ref[peer] = jnp.where(
            lane < HALF, metric_ref[asked_ref[peer, 0]], metric_ref[asked_ref[peer, 1]]
        )


def term_kernel(first, first_slot, owner_ref, halves_ref, metric_ref, *refs):
    *before, out_ref, total = refs
    item_count, rows, _ = halves_ref.shape
    width = total.shape[0] // SLOTS
    depth = metric_ref.shape[1]
    steps = (item_count + 1) // 2
    groups = rows // width
    lane = lax.broadcasted_iota(jnp.int32, (depth, LANES), 1)
    rest = jnp.zeros((HALF - depth, LANES), jnp.float32)

    def placed(item):
        mine = owner_ref[item]
        slot = jnp.int32(0)
        for other in range(item):
            slot = slot | jnp.where(owner_ref[other] == mine, 1, 0)
        block = metric_ref[mine].astype(jnp.float32)
        turned = pltpu.roll(block, HALF, 1)
        low = jnp.where(slot == 0, block, turned)
        high = jnp.where(slot == 0, turned, block)
        stacked = [jnp.where(lane < HALF, low, 0.0), rest, jnp.where(lane < HALF, 0.0, high), rest]
        return jnp.concatenate(stacked, axis=0).astype(jnp.bfloat16)

    def spread(array):
        return jnp.concatenate(
            [array[g * width : (g + 1) * width, :] for g in range(groups)], axis=1
        )

    def term(item):
        if item >= item_count:
            return jnp.zeros((width, HALF), jnp.float32)
        halves = halves_ref[item]
        fitted = jnp.dot(halves, placed(first + item), preferred_element_type=jnp.float32)
        return lax.dot_general(
            spread(halves),
            spread(fitted.astype(jnp.bfloat16)),
            (((1,), (1,)), ((), ())),
            preferred_element_type=jnp.float32,
        )

    total[...] = before[0][...] if before else jnp.zeros_like(total)
    for step in range(steps):
        total[pl.ds(first_slot + step, width, stride=SLOTS), :] = jnp.concatenate(
            [term(step), term(step + steps)], axis=1
        )
    out_ref[...] = total[...].astype(out_ref.dtype)


def combine_kernel(parts_ref, pick_ref, out_ref, sum_ref):
    sources = parts_ref.shape[0]
    rows = parts_ref.shape[1] // SLOTS
    pairs = pick_ref.shape[0] // 8
    low = lax.broadcasted_iota(jnp.int32, (pairs, LANES), 1) < HALF
    for step in range(rows // 2):
        block = parts_ref[:, step * 2 * SLOTS : (step + 1) * 2 * SLOTS, :]
        summed = jnp.dot(
            pick_ref[...],
            block.reshape(sources * 2 * SLOTS, LANES),
            preferred_element_type=jnp.float32,
        )
        for parity in range(2):
            at = parity * 4 * pairs
            even = summed[at : at + pairs] + pltpu.roll(summed[at + pairs : at + 2 * pairs], HALF, 1)
            odd = summed[at + 3 * pairs : at + 4 * pairs] + pltpu.roll(
                summed[at + 2 * pairs : at + 3 * pairs], HALF, 1
            )
            sum_ref[pl.ds(step * 2 + parity, pairs, stride=rows), :] = jnp.where(low, even, odd)
    out_ref[...] = sum_ref[...].astype(out_ref.dtype)


def final_kernel(parts_ref, out_ref):
    rows = out_ref.shape[1]
    parts = parts_ref[...].astype(jnp.float32)
    step = 8 // rows * rows
    summed = parts[:step]
    for at in range(step, parts.shape[0], step):
        summed = summed + parts[at : at + step]
    summed = sum(summed[at : at + rows] for at in range(0, step, rows))
    for side in range(out_ref.shape[0]):
        out_ref[side] = summed[:, side * HALF : (side + 1) * HALF]


def shards(tiles, coeff, support, row_block, col_block, owner, local_block, metric):
    item_count, width, columns = tiles.shape
    aux_width = metric.shape[1]
    orbitals = support.shape[1]
    aux_count = lax.axis_size("aux")
    pair_count = lax.axis_size("pair")
    groups = orbitals // 2
    vmem = pl.BlockSpec(memory_space=pltpu.VMEM)
    smem = pl.BlockSpec(memory_space=pltpu.SMEM)
    anywhere = pl.BlockSpec(memory_space=pl.ANY)
    small = pltpu.CompilerParams(vmem_limit_bytes=8 * MIB)
    row = lambda array: array.reshape(1, item_count)

    request = pl.pallas_call(
        request_kernel,
        out_shape=jax.ShapeDtypeStruct((aux_count, LANES), jnp.int32),
        in_specs=[vmem] * 3,
        out_specs=vmem,
        name="request",
    )(row(owner), row(local_block), row(col_block))
    asked = lax.all_to_all(
        request.reshape(aux_count, 1, LANES), "aux", split_axis=0, concat_axis=0, tiled=True
    ).reshape(aux_count, LANES)

    late_rows = groups * width
    by_aux = metric.transpose(1, 0, 2)
    depth = -(-aux_width // 8) * 8
    early_count = item_count * 3 // 11
    late_count = item_count - early_count

    def half_scratch(count):
        return [
            pltpu.VMEM((count, width, columns), jnp.bfloat16),
            pltpu.VMEM((2, orbitals, columns), jnp.float32),
            pltpu.VMEM((2, late_rows, LANES), jnp.float32),
            pltpu.SemaphoreType.DMA((2 * count + 2,)),
        ]

    def cost(count):
        return pl.CostEstimate(
            flops=2 * count * orbitals * width * columns,
            bytes_accessed=2 * count * (width * columns + late_rows * LANES),
            transcendentals=0,
        )

    padded_shape = (metric.shape[0], depth, LANES)
    picked_shape = (support.shape[0], orbitals, width)
    padded, picked = pl.pallas_call(
        place_kernel,
        out_shape=[
            jax.ShapeDtypeStruct(padded_shape, jnp.bfloat16),
            jax.ShapeDtypeStruct((ROOM,) + picked_shape[1:], jnp.bfloat16),
        ],
        in_specs=[smem] + [vmem] * 3,
        out_specs=[vmem, anywhere],
        scratch_shapes=[
            pltpu.VMEM(picked_shape, jnp.bfloat16),
            pltpu.VMEM((item_count,) + picked_shape[1:], jnp.bfloat16),
            pltpu.VMEM((aux_width * metric.shape[0], LANES), jnp.float32),
            pltpu.SemaphoreType.DMA,
        ],
        compiler_params=pltpu.CompilerParams(vmem_limit_bytes=EARLY_LIMIT),
        name="place",
    )(row_block, by_aux, coeff, support)

    early = pl.pallas_call(
        early_kernel,
        out_shape=jax.ShapeDtypeStruct((early_count, late_rows, LANES), jnp.bfloat16),
        in_specs=[anywhere, anywhere],
        out_specs=anywhere,
        scratch_shapes=[
            pltpu.VMEM((early_count,) + picked_shape[1:], jnp.bfloat16),
            pltpu.VMEM((early_count, late_rows, LANES), jnp.bfloat16),
        ]
        + half_scratch(early_count),
        compiler_params=pltpu.CompilerParams(vmem_limit_bytes=TILES_LIMIT),
        cost_estimate=pl.CostEstimate(
            flops=3 * 10**9, bytes_accessed=4 * 10**6, transcendentals=0
        ),
        name="early",
    )(tiles, picked)

    served = pl.pallas_call(
        serve_kernel,
        out_shape=jax.ShapeDtypeStruct((aux_count, depth, LANES), jnp.bfloat16),
        in_specs=[smem, vmem],
        out_specs=vmem,
        compiler_params=pltpu.CompilerParams(vmem_limit_bytes=8 * MIB),
        name="serve",
    )(asked, padded)
    metric_tiles = lax.all_to_all(served, "aux", split_axis=0, concat_axis=0, tiled=True)

    picked, _ = lax.optimization_barrier((picked, served))
    late = pl.pallas_call(
        late_kernel,
        out_shape=jax.ShapeDtypeStruct((late_count, late_rows, LANES), jnp.bfloat16),
        in_specs=[anywhere, anywhere],
        out_specs=vmem,
        scratch_shapes=[pltpu.VMEM((late_count,) + picked_shape[1:], jnp.bfloat16)]
        + half_scratch(late_count),
        compiler_params=pltpu.CompilerParams(vmem_limit_bytes=LATE_LIMIT),
        cost_estimate=cost(late_count),
        name="late",
    )(tiles, picked)

    cols = asked[:, 32 : 32 + item_count]
    late_steps, early_steps = (late_count + 1) // 2, (early_count + 1) // 2

    def columns_of(*parts):
        taken = []
        for start, stop, size in parts:
            fill = ((0, 0), (0, size - (stop - start)))
            taken.append(jnp.pad(cols[:, start:stop], fill, constant_values=-1))
        return jnp.concatenate(taken, axis=1)

    spare = SLOTS - late_steps
    cols_a = columns_of(
        (0, late_steps, late_steps), (late_count, late_count + early_steps, spare)
    )
    cols_b = columns_of(
        (late_steps, late_count, late_steps), (late_count + early_steps, item_count, spare)
    )
    spread = lambda array: jnp.broadcast_to(array[:, None, :], (aux_count, 2, SLOTS)).reshape(1, -1)
    place = jnp.arange(8 * pair_count, dtype=jnp.int32)[:, None]
    block = 2 * (place % pair_count) + place // (2 * pair_count) % 2
    side_b = place // pair_count % 2 == 1
    parity = jnp.arange(aux_count * 2 * SLOTS, dtype=jnp.int32)[None, :] // SLOTS % 2
    hit = jnp.where(side_b, spread(cols_b) == block, spread(cols_a) == block)
    pick = jnp.where(hit & (parity == place // (4 * pair_count)), -1.0, 0.0).astype(jnp.bfloat16)

    def terms(first, first_slot, halves, before, dtype, name):
        return pl.pallas_call(
            functools.partial(term_kernel, first, first_slot),
            out_shape=jax.ShapeDtypeStruct((width * SLOTS, LANES), dtype),
            in_specs=[smem] + [vmem] * (2 + len(before)),
            out_specs=vmem,
            scratch_shapes=[pltpu.VMEM((width * SLOTS, LANES), jnp.float32)],
            compiler_params=pltpu.CompilerParams(vmem_limit_bytes=TERM_LIMIT),
            cost_estimate=pl.CostEstimate(
                flops=12 * halves.shape[0] * late_rows * LANES * (LANES + width),
                bytes_accessed=2 * halves.size,
                transcendentals=0,
            ),
            name=name,
        )(owner.reshape(item_count), halves, metric_tiles, *before)

    blocks = terms(0, 0, late, (), jnp.float32, "late_term")
    blocks = terms(late_count, late_steps, early, (blocks,), jnp.bfloat16, "early_term")
    rows = width // aux_count
    blocks, pick = lax.optimization_barrier((blocks, pick))
    parts = lax.all_to_all(
        blocks.reshape(aux_count, rows * SLOTS, LANES), "aux", split_axis=0, concat_axis=0, tiled=True
    )

    sums = pl.pallas_call(
        combine_kernel,
        out_shape=jax.ShapeDtypeStruct((pair_count * rows, LANES), jnp.bfloat16),
        in_specs=[vmem] * 2,
        out_specs=vmem,
        scratch_shapes=[pltpu.VMEM((pair_count * rows, LANES), jnp.float32)],
        compiler_params=small,
        name="combine",
    )(parts, pick)
    arrived = lax.all_to_all(
        sums.reshape(pair_count, rows, LANES), "pair", split_axis=0, concat_axis=0, tiled=True
    )
    return pl.pallas_call(
        final_kernel,
        out_shape=jax.ShapeDtypeStruct((2, rows, width), jnp.float32),
        in_specs=[vmem],
        out_specs=vmem,
        compiler_params=small,
        name="final",
    )(arrived.reshape(pair_count * rows, LANES))


def solution(mesh):
    return jax.shard_map(
        shards,
        mesh=mesh,
        in_specs=(
            P(("pair", "aux"), None, None),
            P("pair", None),
            P("pair", None),
            P(("pair", "aux")),
            P(("pair", "aux")),
            P(("pair", "aux"), None),
            P(("pair", "aux")),
            P("aux", None, None),
        ),
        out_specs=P("pair", "aux", None),
        check_vma=False,
    )
```
